256 devices in a mesh: dp: 4 (over y), expert: 64 (over z, x, core).
Axes of the slice: x: 4, y: 4, z: 8, core: 2. Of those that a mesh axis runs over, the one named last changes fastest.
Arguments:
- grad_parts: bfloat16 [4, 512, 1536, 256], P('dp', None, 'expert'), may hold values from -6 to 6
- momentum: bfloat16 [512, 1536, 256], P('dp', 'expert'), may hold values from -6 to 6
- block_ids: int32 [512], P('dp'), may hold values from 0 to 511, each once
- step: int32 [1], replicated, may hold values from 0 to 9999
- logit_max: float32 [4, 64, 4, 64], P('dp', 'expert'), may hold values from 5 to 600, as said below
Outputs:
- new_momentum: bfloat16 [512, 1536, 256], P('dp', 'expert')
- update: bfloat16 [512, 1536, 256], P('dp', 'expert')
- clip_scale: float32 [512, 256], P('dp')
The draws below stay inside these ranges and needn't reach their ends.
Inputs may be any that keep to these rules, and one draw needn't show every extreme that they name: `block_ids`: every slot number appears once. `logit_max`: positive.
All inputs are finite; a program needn't handle non-finite values.
Results may differ from the reference program's by a relative error of at most 0.02.
Values may be sent and summed in bfloat16 or wider, within the bound.
A program may use at most 64 MiB of HBM per device.

```python
import jax
import jax.numpy as jnp
from jax import lax

HEADS = 64
Q_IN = 1536
KV_IN = 512
NOPE_DIM = 128
NS_STEPS = 5
Q_OUT = 192
KV_OUT = 256
MATS = 512
LAYERS_WIN = 4
N_DP = 4
N_EXPERT = 64


def draw_grad_parts(key, part):
    key = jax.random.fold_in(key, 11)
    row_key = jax.random.fold_in(key, 0)
    col_key = jax.random.fold_in(key, 1)
    own_key = jax.random.fold_in(key, 3)
    row_scale = jnp.exp(jax.random.uniform(row_key, (1, 1, Q_IN, 1), jnp.float32) * jnp.log(3.2))
    col_scale = jnp.exp(jax.random.uniform(col_key, (1, 1, 1, KV_OUT), jnp.float32) * jnp.log(3.2))
    values = jax.random.truncated_normal(own_key, -3.9, 3.9, (N_DP, MATS, Q_IN, KV_OUT), jnp.float32)
    return (0.15 * values * row_scale * col_scale).astype(jnp.bfloat16)


def draw_logit_max(key, part):
    key = jax.random.fold_in(key, 23)
    ground_key, device_key, spike_key, mode_key, row_key, near_key, level_key = jax.random.split(key, 7)
    devices = N_DP * N_EXPERT
    position = (jnp.arange(devices, dtype=jnp.float32) / max(devices - 1, 1)).reshape(N_DP, N_EXPERT, 1, 1)
    ground = jax.random.uniform(ground_key, (N_DP, N_EXPERT, LAYERS_WIN, HEADS), jnp.float32, 5.0, 15.0) * (1.0 + 2.0 * position)
    chosen = jax.random.randint(device_key, (LAYERS_WIN, HEADS), 0, devices)
    hot_row = jax.random.randint(row_key, (LAYERS_WIN, HEADS), 0, N_DP)
    spread_head = jax.random.randint(mode_key, (LAYERS_WIN, HEADS), 0, 2) == 1
    near = jax.random.uniform(near_key, (N_DP, N_EXPERT, LAYERS_WIN, HEADS), jnp.float32, 0.97, 1.0)
    spike = jnp.exp(jax.random.uniform(spike_key, (LAYERS_WIN, HEADS), jnp.float32, jnp.log(101.0), jnp.log(600.0)))
    level = jnp.exp(jax.random.uniform(level_key, (LAYERS_WIN, HEADS), jnp.float32, jnp.log(104.0), jnp.log(145.0)))
    holder = jnp.arange(devices).reshape(N_DP, N_EXPERT, 1, 1) == chosen[None, None]
    in_row = jnp.arange(N_DP).reshape(N_DP, 1, 1, 1) == hot_row[None, None]
    single = jnp.where(holder, jnp.maximum(spike, ground), ground)
    spread = jnp.where(in_row, level[None, None] * near, ground)
    return jnp.where(spread_head[None, None], spread, single)


def block_scale(key, shape, cuts, least, top_value):
    def one(dim, parts):
        steps = jax.random.uniform(jax.random.fold_in(jax.random.fold_in(key, 6), dim), (parts,), jnp.float32, least / len(cuts), top_value / len(cuts))
        return jnp.repeat(jnp.exp(steps), shape[dim] // parts).reshape((-1,) + (1,) * (len(shape) - dim - 1))

    level = one(*cuts[0])
    for cut in cuts[1:]:
        level = level * one(*cut)
    return level


def centred(key, shape, scale, most, cuts=(), kind=jnp.bfloat16):
    result = scale * jax.random.normal(key, shape, jnp.float32)
    if cuts:
        result = result * block_scale(key, shape, cuts, -0.22, 0.18)
    return jnp.clip(result, -most, most).astype(kind)


def setup_inputs(seed: int = 0) -> dict:
    key_of = jax.random.split(jax.random.key(seed), 6)
    return {
        "grad_parts": draw_grad_parts(jax.random.fold_in(key_of[5], 71), 0),
        "momentum": centred(key_of[1], (MATS, Q_IN, KV_OUT), 1.5, 6.0, ((0, 4), (1, 64))),
        "block_ids": jax.random.permutation(key_of[2], MATS).astype(jnp.int32),
        "step": jax.random.randint(key_of[3], (1,), 0, 10000).astype(jnp.int32),
        "logit_max": draw_logit_max(jax.random.fold_in(key_of[5], 71), 0),
    }


quintic_a = 3.4445
quintic_b = -4.775
quintic_c = 2.0315
norm_eps = 1e-07
beta_coef = 0.95
clip_tau = 100.0
plan_span = 10000.0
rms_match = 0.2
full_prec = lax.Precision.HIGHEST

def orthogonalize(direction):
    values = direction.astype(jnp.float32)
    squares = jnp.sum(jnp.square(values))
    current = values / (jnp.sqrt(squares) + norm_eps)
    for sweep_index in range(NS_STEPS):
        gram_matrix = lax.dot_general(current, current, (((0,), (0,)), ((), ())), precision=full_prec, preferred_element_type=jnp.float32)
        polynomial = quintic_b * gram_matrix + quintic_c * jnp.dot(gram_matrix, gram_matrix, precision=full_prec, preferred_element_type=jnp.float32)
        current = quintic_a * current + jnp.dot(current, polynomial, precision=full_prec, preferred_element_type=jnp.float32)
    return current

def query_branch(direction):
    return jnp.pad(orthogonalize(direction[:, :Q_OUT]), ((0, 0), (0, KV_OUT - Q_OUT)))

def value_branch(direction):
    return jnp.pad(orthogonalize(direction[:KV_IN, :]), ((0, Q_IN - KV_IN), (0, 0)))

def slot_step(replica_parts, held_state, block_id, step_rate):
    block_kind = block_id % 2
    in_live = jnp.where(block_kind == 0, Q_IN, KV_IN)
    out_live = jnp.where(block_kind == 0, Q_OUT, KV_OUT)
    live_mask = (jnp.arange(Q_IN)[:, None] < in_live) & (jnp.arange(KV_OUT)[None, :] < out_live)
    gradient = jnp.where(live_mask, lax.optimization_barrier(jnp.sum(replica_parts.astype(jnp.float32), axis=0)), 0.0)
    fresh_state = jnp.where(live_mask, beta_coef * held_state.astype(jnp.float32) + gradient, 0.0).astype(jnp.bfloat16)
    nesterov = (gradient + beta_coef * fresh_state.astype(jnp.float32)).astype(jnp.bfloat16)
    orthogonal = lax.cond(block_kind == 0, query_branch, value_branch, nesterov)
    widest = jnp.where(block_kind == 0, max(Q_IN, Q_OUT), max(KV_IN, KV_OUT))
    factor = step_rate * rms_match * jnp.sqrt(widest.astype(jnp.float32))
    update = (factor * orthogonal).astype(jnp.bfloat16)
    return (fresh_state, update)

def reference(grad_parts, momentum, block_ids, step, logit_max):
    step_rate = 0.1 + 0.45 * (1.0 + jnp.cos(jnp.pi * step[0].astype(jnp.float32) / plan_span))
    stacked = jnp.moveaxis(grad_parts, 1, 0)
    new_momentum, update = lax.map(lambda slot_items: slot_step(slot_items[0], slot_items[1], slot_items[2], step_rate), (stacked, momentum, block_ids))
    head_peaks = lax.optimization_barrier(jnp.max(logit_max, axis=(0, 1)))
    clip_eta = jnp.minimum(1.0, clip_tau / head_peaks).reshape(-1)
    slot_eta = clip_eta[block_ids // 2]
    out_rows = jnp.arange(KV_OUT)[None, :]
    root_eta = jnp.sqrt(slot_eta)[:, None]
    query_rows = jnp.where(out_rows < NOPE_DIM, root_eta, jnp.where(out_rows < Q_OUT, slot_eta[:, None], 0.0))
    value_rows = jnp.where(out_rows < NOPE_DIM, root_eta, 1.0)
    clip_scale = jnp.where((block_ids % 2 == 0)[:, None], query_rows, value_rows)
    return (new_momentum, update, clip_scale)
```

```python
import functools
import jax
import jax.numpy as jnp
from jax import lax
from jax.experimental import pallas as pl
from jax.experimental.pallas import tpu as pltpu
from jax.sharding import PartitionSpec as P

Q_IN = 1536
KV_IN = 512
NOPE_DIM = 128
NS_STEPS = 5
Q_OUT = 192
KV_OUT = 256

quintic_a = 3.4445
quintic_b = -4.775
quintic_c = 2.0315
norm_eps = 1e-07
beta_coef = 0.95
clip_tau = 100.0
plan_span = 10000.0
rms_match = 0.2


def split(value):
    high = value.astype(jnp.bfloat16)
    low = (value - high.astype(jnp.float32)).astype(jnp.bfloat16)
    return high, low


def dot(left, right):
    return jnp.dot(left, right, preferred_element_type=jnp.float32)


def product(left, right):
    (lh, ll), (rh, rl) = left, right
    return dot(lh, rh) + (dot(lh, rl) + dot(ll, rh))


def polar_factor(gram0):
    rows = lax.broadcasted_iota(jnp.int32, gram0.shape, 0)
    columns = lax.broadcasted_iota(jnp.int32, gram0.shape, 1)
    eye = jnp.where(rows == columns, 1.0, 0.0)
    squares = jnp.sum(jnp.sum(gram0 * eye, axis=1, keepdims=True), axis=0, keepdims=True)
    inverse = 1.0 / (jnp.sqrt(squares) + norm_eps)
    gram = (gram0 * inverse) * inverse
    factor = None
    for sweep in range(NS_STEPS):
        parts = split(gram)
        poly = quintic_a * eye + quintic_b * gram + quintic_c * product(parts, parts)
        poly_parts = split(poly)
        factor = poly if factor is None else product(split(factor), poly_parts)
        if sweep < NS_STEPS - 1:
            gram = product(split(product(parts, poly_parts)), poly_parts)
    return factor * inverse


def ns_kernel(scale_ref, rows_ref, out_ref):
    block = rows_ref[...].reshape(64, 24, KV_OUT).astype(jnp.float32)
    rows = block.reshape(Q_IN, KV_OUT).astype(jnp.bfloat16)
    gram0 = lax.dot_general(rows, rows, (((0,), (0,)), ((), ())), preferred_element_type=jnp.float32)
    factor = polar_factor(gram0) * scale_ref[pl.program_id(0)]
    high, low = split(factor)
    update = dot(rows, high) + dot(rows, low)
    out_ref[...] = update.reshape(64, 1, 24, KV_OUT).astype(jnp.bfloat16)


def newton_schulz(rows, scales):
    return pl.pallas_call(
        ns_kernel,
        grid=(2,),
        in_specs=[
            pl.BlockSpec(memory_space=pltpu.SMEM),
            pl.BlockSpec((64, 1, 24, KV_OUT), lambda i: (0, i, 0, 0)),
        ],
        out_specs=pl.BlockSpec((64, 1, 24, KV_OUT), lambda i: (0, i, 0, 0)),
        out_shape=jax.ShapeDtypeStruct((64, 2, 24, KV_OUT), jnp.bfloat16),
        compiler_params=pltpu.CompilerParams(vmem_limit_bytes=48 * 2**20),
    )(scales, rows)


def live_limits(block_kind):
    in_live = jnp.where(block_kind == 0, Q_IN, KV_IN)
    out_live = jnp.where(block_kind == 0, Q_OUT, KV_OUT)
    return (in_live, out_live)


def body(grad_parts, momentum, block_ids, step, logit_max):
    owners = lax.axis_size("expert")
    column = lax.axis_index("expert")
    slot_rows = momentum.shape[0]
    piece_rows = momentum.shape[1]
    slots_each = slot_rows // owners
    head_peaks = jnp.max(lax.all_gather(logit_max[0, 0], ("dp", "expert"), axis=0, tiled=False), axis=0)
    summed = lax.psum_scatter(
        grad_parts[0], "dp", scatter_dimension=0, tiled=True
    ).astype(jnp.float32)
    step_rate = 0.1 + 0.45 * (1.0 + jnp.cos(jnp.pi * step[0].astype(jnp.float32) / plan_span))
    block_kind = block_ids % 2
    in_live, out_live = live_limits(block_kind)
    in_pos = column * piece_rows + jnp.arange(piece_rows)
    live_mask = (in_pos[None, :, None] < in_live[:, None, None]) & (
        jnp.arange(KV_OUT)[None, None, :] < out_live[:, None, None]
    )
    gradient = jnp.where(live_mask, summed, 0.0)
    fresh = jnp.where(live_mask, beta_coef * momentum.astype(jnp.float32) + gradient, 0.0).astype(jnp.bfloat16)
    nesterov = (gradient + beta_coef * fresh.astype(jnp.float32)).astype(jnp.bfloat16)
    own_kind = lax.dynamic_slice_in_dim(block_kind, column * slots_each, slots_each, 0)
    widest = jnp.where(own_kind == 0, max(Q_IN, Q_OUT), max(KV_IN, KV_OUT))
    scales = step_rate * rms_match * jnp.sqrt(widest.astype(jnp.float32))
    own = lax.all_to_all(nesterov, "expert", split_axis=0, concat_axis=0, tiled=True)
    update_own = newton_schulz(own.reshape(owners, slots_each, piece_rows, KV_OUT), scales)
    update_rows = lax.all_to_all(
        update_own.reshape(slot_rows, piece_rows, KV_OUT), "expert", split_axis=0, concat_axis=0, tiled=True
    )
    clip_eta = jnp.minimum(1.0, clip_tau / head_peaks).reshape(-1)
    head_pair = block_ids // 2
    picker = head_pair[:, None] == jnp.arange(clip_eta.shape[0])[None, :]
    slot_eta = jnp.sum(jnp.where(picker, clip_eta[None, :], 0.0), axis=1)
    out_rows = jnp.arange(KV_OUT)[None, :]
    root_eta = jnp.sqrt(slot_eta)[:, None]
    query_rows = jnp.where(
        out_rows < NOPE_DIM, root_eta, jnp.where(out_rows < Q_OUT, slot_eta[:, None], 0.0)
    )
    value_rows = jnp.where(out_rows < NOPE_DIM, root_eta, 1.0)
    clip_scale = jnp.where((block_kind == 0)[:, None], query_rows, value_rows)
    return (fresh, update_rows, clip_scale)


def solution(mesh):
    in_specs = (
        P("dp", None, "expert", None),
        P("dp", "expert", None),
        P("dp"),
        P(),
        P("dp", "expert", None, None),
    )
    out_specs = (P("dp", "expert", None), P("dp", "expert", None), P("dp", None))
    return jax.shard_map(body, mesh=mesh, in_specs=in_specs, out_specs=out_specs, check_vma=False)
```

```python
import math

import jax
import jax.numpy as jnp
from jax import lax
from jax.experimental import pallas as pl
from jax.experimental.pallas import tpu as pltpu
from jax.sharding import PartitionSpec as P

Q_IN = 1536
KV_IN = 512
NOPE_DIM = 128
NS_STEPS = 5
Q_OUT = 192
KV_OUT = 256
ROWS = 24
SLOTS = 128
ROUNDS = 4
PER = 32
HALF = 16
Z = 8
X = 4
DP = 4
MESH = pl.DeviceIdType.MESH

quintic_a = 3.4445
quintic_b = -4.775
quintic_c = 2.0315
norm_eps = 1e-07
beta_coef = 0.95
clip_tau = 100.0
plan_span = 10000.0
rms_match = 0.2
QUERY_SCALE = rms_match * math.sqrt(max(Q_IN, Q_OUT))
VALUE_SCALE = rms_match * math.sqrt(max(KV_IN, KV_OUT))


def split(value):
    high = value.astype(jnp.bfloat16)
    low = (value - high.astype(jnp.float32)).astype(jnp.bfloat16)
    return high, low


def dot(left, right):
    return jnp.dot(left, right, preferred_element_type=jnp.float32)


def product(left, right):
    (lh, ll), (rh, rl) = left, right
    return dot(lh, rh) + (dot(lh, rl) + dot(ll, rh))


def polar_factor(gram0):
    rows = lax.broadcasted_iota(jnp.int32, gram0.shape, 0)
    columns = lax.broadcasted_iota(jnp.int32, gram0.shape, 1)
    eye = jnp.where(rows == columns, 1.0, 0.0)
    squares = jnp.sum(jnp.sum(gram0 * eye, axis=1, keepdims=True), axis=0, keepdims=True)
    inverse = 1.0 / (jnp.sqrt(squares) + norm_eps)
    gram = (gram0 * inverse) * inverse
    factor = None
    for sweep in range(NS_STEPS):
        parts = split(gram)
        poly = quintic_a * eye + quintic_b * gram + quintic_c * product(parts, parts)
        poly_parts = split(poly)
        factor = poly if factor is None else product(split(factor), poly_parts)
        if sweep < NS_STEPS - 1:
            gram = product(split(product(parts, poly_parts)), poly_parts)
    return factor * inverse


def step_kernel(
    ids_ref, rate_ref, grads, momentum, logit, fresh_out, update_out, peaks_out,
    own, near_up, near_down, held, relay_up, relay_down, in_up, in_down, nest, fresh, owned, back,
    peak_dp, peak_row, peak_col, peak_a, peak_b,
    load_sem, relay_send, relay_sem, raw_send, sum_send, in_sem, go_send, go_sem, back_send, back_sem, fresh_sem,
    peak_send, peak_sem,
):
    d = lax.axis_index("dp")
    e = lax.axis_index("expert")
    z, x, core = e // (2 * X), (e // 2) % X, e % 2
    place = e // 2
    up, down, far = (d + 1) % DP, (d + 3) % DP, (d + 2) % DP

    def shifted(k):
        return ((z + k % Z) % Z) * X + (x + k // Z) % X

    def remote(source, target, send, recv, where):
        return pltpu.make_async_remote_copy(
            src_ref=source, dst_ref=target, send_sem=send, recv_sem=recv, device_id=where, device_id_type=MESH
        )

    def drain(ref, sem):
        pltpu.make_async_copy(ref, ref, sem).wait()

    loads = [
        pltpu.make_async_copy(grads.at[up, :, 0], near_up, load_sem.at[0]),
        pltpu.make_async_copy(grads.at[down, :, 1], near_down, load_sem.at[1]),
        pltpu.make_async_copy(grads.at[d], own, load_sem.at[2]),
        pltpu.make_async_copy(momentum, held, load_sem.at[3]),
    ]
    for load in loads:
        load.start()

    barrier = pltpu.get_barrier_semaphore()

    def greet(k, _):
        pl.semaphore_signal(barrier, inc=1, device_id=(d, (e + k) % (2 * X * Z)), device_id_type=MESH)
        return 0

    for other in (up, down, far):
        pl.semaphore_signal(barrier, inc=1, device_id=(other, e), device_id_type=MESH)
    lax.fori_loop(1, 2 * X * Z, greet, 0)
    pl.semaphore_wait(barrier, 2 * X * Z + 2)

    def relay(r):
        remote(grads.at[far, r, 0], relay_down.at[r], relay_send, relay_sem.at[r, 0], (up, e)).start()
        remote(grads.at[far, r, 1], relay_up.at[r], relay_send, relay_sem.at[r, 1], (down, e)).start()

    def raw(r):
        remote(grads.at[up, r, 1], in_down.at[r, 1], raw_send, in_sem.at[r, 0], (up, e)).start()
        remote(grads.at[down, r, 0], in_up.at[r, 0], raw_send, in_sem.at[r, 1], (down, e)).start()

    def combine(r):
        for side, (near, relayed) in enumerate(((near_up, relay_down), (near_down, relay_up))):
            drain(relayed.at[r], relay_sem.at[r, side])

            def add(i, _, near=near, relayed=relayed):
                near[r, i] = (near[r, i].astype(jnp.float32) + relayed[r, i].astype(jnp.float32)).astype(jnp.bfloat16)
                return 0

            lax.fori_loop(0, HALF, add, 0)
            if side == 0:
                remote(near_up.at[r], in_down.at[r, 0], sum_send, in_sem.at[r, 0], (up, e)).start()
            else:
                remote(near_down.at[r], in_up.at[r, 1], sum_send, in_sem.at[r, 1], (down, e)).start()

    row = e * ROWS + lax.broadcasted_iota(jnp.int32, (ROWS, KV_OUT), 0)
    column = lax.broadcasted_iota(jnp.int32, (ROWS, KV_OUT), 1)
    query_live = jnp.where(column < Q_OUT, 1.0, 0.0)
    value_live = jnp.where(row < KV_IN, 1.0, 0.0)

    def home(r):
        drain(in_down.at[r], in_sem.at[r, 0])
        drain(in_up.at[r], in_sem.at[r, 1])
        for half in range(2):

            def one(i, _, half=half):
                slot = r * PER + half * HALF + i
                query = (1 - ids_ref[slot] % 2).astype(jnp.float32)
                live = value_live + query * (query_live - value_live)
                total = own[r, half, i].astype(jnp.float32) + (
                    in_down[r, half, i].astype(jnp.float32) + in_up[r, half, i].astype(jnp.float32)
                )
                gradient = live * total
                state = (live * (beta_coef * held[slot].astype(jnp.float32) + gradient)).astype(jnp.bfloat16)
                fresh[slot] = state
                nest[slot] = (gradient + beta_coef * state.astype(jnp.float32)).astype(jnp.bfloat16)
                return 0

            lax.fori_loop(0, HALF, one, 0)
        pltpu.make_async_copy(fresh.at[pl.ds(r * PER, PER)], fresh_out.at[pl.ds(r * PER, PER)], fresh_sem).start()

    def go(r):
        def send(k, _):
            rank = shifted(k)
            target = 2 * rank + r % 2

            @pl.when(target != e)
            def _():
                remote(nest.at[r * PER + rank], owned.at[r // 2, e], go_send.at[r], go_sem.at[r // 2], (d, target)).start()

            @pl.when(target == e)
            def _():
                pltpu.make_async_copy(nest.at[r * PER + rank], owned.at[r // 2, e], go_sem.at[r // 2]).start()

            return 0

        lax.fori_loop(0, PER, send, 0)

    def orthogonalize(j):
        slot = (2 * j + core) * PER + place
        query = (1 - ids_ref[slot] % 2).astype(jnp.float32)
        width = VALUE_SCALE + query * (QUERY_SCALE - VALUE_SCALE)
        drain(owned.at[j], go_sem.at[j])
        block = owned[j].astype(jnp.float32)
        rows = block.reshape(Q_IN, KV_OUT).astype(jnp.bfloat16)
        gram0 = lax.dot_general(rows, rows, (((0,), (0,)), ((), ())), preferred_element_type=jnp.float32)
        factor = polar_factor(gram0) * (width * rate_ref[0])
        high, low = split(factor)
        update = dot(rows, high) + dot(rows, low)
        back[j] = update.reshape(2 * X * Z, ROWS, KV_OUT).astype(jnp.bfloat16)

    def give(j):
        slot = (2 * j + core) * PER + place

        def send(k, _):
            target = 2 * shifted(k // 2) + (core + k % 2) % 2

            @pl.when(target != e)
            def _():
                remote(back.at[j, target], update_out.at[slot], back_send.at[j], back_sem, (d, target)).start()

            @pl.when(target == e)
            def _():
                pltpu.make_async_copy(back.at[j, target], update_out.at[slot], back_sem).start()

            return 0

        lax.fori_loop(0, 2 * X * Z, send, 0)

    for source, side in ((up, 0), (down, 0), (far, 0)):
        remote(logit, peak_dp.at[d], peak_send.at[0], peak_sem.at[0], (source, e)).start()
    pltpu.make_async_copy(logit, peak_dp.at[d], peak_sem.at[0]).start()

    def peaks_row():
        drain(peak_dp, peak_sem.at[0])
        peak_a[...] = jnp.max(peak_dp[...], axis=0)
        inner = 2 * x + core

        def send(k, _):
            remote(peak_a, peak_row.at[inner], peak_send.at[1], peak_sem.at[1], (d, 2 * X * z + (inner + k) % (2 * X))).start()
            return 0

        lax.fori_loop(1, 2 * X, send, 0)
        pltpu.make_async_copy(peak_a, peak_row.at[inner], peak_sem.at[1]).start()

    def peaks_column():
        drain(peak_row, peak_sem.at[1])
        peak_b[...] = jnp.max(peak_row[...], axis=0)

        def send(k, _):
            remote(peak_b, peak_col.at[z], peak_send.at[2], peak_sem.at[2], (d, 2 * X * ((z + k) % Z) + 2 * x + core)).start()
            return 0

        lax.fori_loop(1, Z, send, 0)
        pltpu.make_async_copy(peak_b, peak_col.at[z], peak_sem.at[2]).start()

    relay(0)
    raw(0)
    relay(1)
    raw(1)
    for load in loads:
        load.wait()
    combine(0)
    relay(2)
    raw(2)
    combine(1)
    relay(3)
    raw(3)
    home(0)
    go(0)
    combine(2)
    peaks_row()
    home(1)
    go(1)
    combine(3)
    peaks_column()
    home(2)
    go(2)
    orthogonalize(0)
    give(0)
    home(3)
    go(3)
    orthogonalize(1)
    give(1)

    drain(peak_col, peak_sem.at[2])
    peaks_out[...] = jnp.max(peak_col[...], axis=0)
    drain(peak_dp.at[pl.ds(0, DP - 1)], peak_send.at[0])
    drain(peak_row.at[pl.ds(0, 2 * X - 1)], peak_send.at[1])
    drain(peak_col.at[pl.ds(0, Z - 1)], peak_send.at[2])
    for sem in (relay_send, raw_send, sum_send, fresh_sem):
        drain(fresh, sem)
    for r in range(ROUNDS):

        @pl.when(core == r % 2)
        def _():
            drain(nest.at[pl.ds(0, PER - 1)], go_send.at[r])

        @pl.when(core != r % 2)
        def _():
            drain(nest.at[pl.ds(0, PER)], go_send.at[r])

    for j in range(2):
        drain(back.at[j, pl.ds(0, 2 * X * Z - 1)], back_send.at[j])
    drain(update_out, back_sem)


def fused_step(ids, rate, grads, momentum, logit):
    slab = (ROWS, KV_OUT)
    bf16 = jnp.bfloat16
    halves = pltpu.VMEM((ROUNDS, HALF) + slab, bf16)
    wholes = pltpu.VMEM((ROUNDS, 2, HALF) + slab, bf16)
    slots = pltpu.VMEM((SLOTS,) + slab, bf16)
    pair = pltpu.VMEM((2, 2 * X * Z) + slab, bf16)
    heads = logit.shape
    dma = pltpu.SemaphoreType.DMA
    smem = pl.BlockSpec(memory_space=pltpu.SMEM)
    vmem = pl.BlockSpec(memory_space=pltpu.VMEM)
    anywhere = pl.BlockSpec(memory_space=pl.ANY)
    return pl.pallas_call(
        step_kernel,
        in_specs=[smem, smem, anywhere, anywhere, vmem],
        out_specs=[anywhere, anywhere, vmem],
        out_shape=[
            jax.ShapeDtypeStruct((SLOTS,) + slab, bf16),
            jax.ShapeDtypeStruct((SLOTS,) + slab, bf16),
            jax.ShapeDtypeStruct(heads, jnp.float32),
        ],
        scratch_shapes=[
            wholes, halves, halves, slots, halves, halves, wholes, wholes, slots, slots, pair, pair,
            pltpu.VMEM((DP,) + heads, jnp.float32),
            pltpu.VMEM((2 * X,) + heads, jnp.float32),
            pltpu.VMEM((Z,) + heads, jnp.float32),
            pltpu.VMEM(heads, jnp.float32),
            pltpu.VMEM(heads, jnp.float32),
            dma((4,)), dma, dma((ROUNDS, 2)), dma, dma, dma((ROUNDS, 2)), dma((ROUNDS,)), dma((2,)), dma((2,)), dma, dma,
            dma((3,)), dma((3,)),
        ],
        compiler_params=pltpu.CompilerParams(
            collective_id=0, has_side_effects=True, vmem_limit_bytes=56 * 2**20
        ),
    )(ids, rate, grads, momentum, logit)


def body(grad_parts, momentum, block_ids, step, logit_max):
    step_rate = 0.1 + 0.45 * (1.0 + jnp.cos(jnp.pi * step.astype(jnp.float32) / plan_span))
    grads = grad_parts.reshape(DP, ROUNDS, 2, HALF, ROWS, KV_OUT)
    fresh, update_rows, head_peaks = fused_step(block_ids, step_rate, grads, momentum, logit_max[0, 0])
    clip_eta = jnp.minimum(1.0, clip_tau / head_peaks).reshape(-1)
    block_kind = block_ids % 2
    head_pair = block_ids // 2
    picker = head_pair[:, None] == jnp.arange(clip_eta.shape[0])[None, :]
    slot_eta = jnp.sum(jnp.where(picker, clip_eta[None, :], 0.0), axis=1)
    out_rows = jnp.arange(KV_OUT)[None, :]
    root_eta = jnp.sqrt(slot_eta)[:, None]
    query_rows = jnp.where(
        out_rows < NOPE_DIM, root_eta, jnp.where(out_rows < Q_OUT, slot_eta[:, None], 0.0)
    )
    value_rows = jnp.where(out_rows < NOPE_DIM, root_eta, 1.0)
    clip_scale = jnp.where((block_kind == 0)[:, None], query_rows, value_rows)
    return (fresh, update_rows, clip_scale)


def solution(mesh):
    in_specs = (
        P("dp", None, "expert", None),
        P("dp", "expert", None),
        P("dp"),
        P(),
        P("dp", "expert", None, None),
    )
    out_specs = (P("dp", "expert", None), P("dp", "expert", None), P("dp", None))
    return jax.shard_map(body, mesh=mesh, in_specs=in_specs, out_specs=out_specs, check_vma=False)
```

```python
import math

import jax
import jax.numpy as jnp
from jax import lax
from jax.experimental import pallas as pl
from jax.experimental.pallas import tpu as pltpu
from jax.sharding import PartitionSpec as P

Q_IN = 1536
KV_IN = 512
NOPE_DIM = 128
NS_STEPS = 5
Q_OUT = 192
KV_OUT = 256
ROWS = 24
SLOTS = 128
ROUNDS = 8
PER = 16
HALF = 8
LAG = 2
PACE = 12
Z = 8
X = 4
DP = 4
MESH = pl.DeviceIdType.MESH

quintic_a = 3.4445
quintic_b = -4.775
quintic_c = 2.0315
norm_eps = 1e-07
beta_coef = 0.95
clip_tau = 100.0
plan_span = 10000.0
rms_match = 0.2
QUERY_SCALE = rms_match * math.sqrt(max(Q_IN, Q_OUT))
VALUE_SCALE = rms_match * math.sqrt(max(KV_IN, KV_OUT))


def split(value):
    high = value.astype(jnp.bfloat16)
    low = (value - high.astype(jnp.float32)).astype(jnp.bfloat16)
    return high, low


def dot(left, right):
    return jnp.dot(left, right, preferred_element_type=jnp.float32)


def product(left, right):
    (lh, ll), (rh, rl) = left, right
    return dot(lh, rh) + (dot(lh, rl) + dot(ll, rh))


def polar_factor(gram0):
    rows = lax.broadcasted_iota(jnp.int32, gram0.shape, 0)
    columns = lax.broadcasted_iota(jnp.int32, gram0.shape, 1)
    eye = jnp.where(rows == columns, 1.0, 0.0)
    squares = jnp.sum(jnp.sum(gram0 * eye, axis=1, keepdims=True), axis=0, keepdims=True)
    inverse = 1.0 / (jnp.sqrt(squares) + norm_eps)
    gram = (gram0 * inverse) * inverse
    factor = None
    for sweep in range(NS_STEPS):
        parts = split(gram)
        poly = quintic_a * eye + quintic_b * gram + quintic_c * product(parts, parts)
        poly_parts = split(poly)
        factor = poly if factor is None else product(split(factor), poly_parts)
        if sweep < NS_STEPS - 1:
            gram = product(split(product(parts, poly_parts)), poly_parts)
    return factor * inverse


def drain(ref, sem):
    pltpu.make_async_copy(ref, ref, sem).wait()


def step_kernel(
    ids_hbm, step_ref, grads, momentum, logit_hbm, fresh, update, peaks_out,
    ids_ref, logit,
    own, near_up, near_down, held, relay_up, relay_down, in_up, in_down, nest, owned, back,
    peak_row, peak_col, peak_dp, peak_a, peak_b,
    load_sem, relay_send, relay_sem, raw_send, sum_send, in_sem, go_send, go_sem, back_send, back_sem,
    peak_send, peak_sem,
):
    d = lax.axis_index("dp")
    e = lax.axis_index("expert")
    z, x, core = e // (2 * X), (e // 2) % X, e % 2
    inner = e % (2 * X)
    family = 2 * ((x + z) % 2) + core
    place = 2 * z + x // 2
    up, down, far = (d + 1) % DP, (d + 3) % DP, (d + 2) % DP

    def remote(source, target, send, recv, where):
        return pltpu.make_async_remote_copy(
            src_ref=source, dst_ref=target, send_sem=send, recv_sem=recv, device_id=where, device_id_type=MESH
        )

    def row_peer(k):
        return 2 * X * z + (inner + k) % (2 * X)

    def column_peer(k):
        return 2 * X * ((z + k) % Z) + inner

    barrier = pltpu.get_barrier_semaphore()

    def greet(where):
        pl.semaphore_signal(barrier, inc=1, device_id=where, device_id_type=MESH)

    for other in (up, down, far):
        greet((other, e))
    for k in range(1, 2 * X):
        greet((d, row_peer(k)))
    for k in range(1, Z):
        greet((d, column_peer(k)))
    loads = [
        pltpu.make_async_copy(grads.at[up, :, 0], near_up, load_sem.at[0]),
        pltpu.make_async_copy(grads.at[down, :, 1], near_down, load_sem.at[1]),
        pltpu.make_async_copy(grads.at[d], own, load_sem.at[2]),
        pltpu.make_async_copy(momentum, held, load_sem.at[3]),
        pltpu.make_async_copy(ids_hbm, ids_ref, load_sem.at[4]),
    ]
    load_logit = pltpu.make_async_copy(logit_hbm, logit, load_sem.at[5])
    load_logit.start()
    for load in loads:
        load.start()
    pl.semaphore_wait(barrier, DP - 1 + 2 * X - 1 + Z - 1)

    def relay(r):
        remote(grads.at[far, r, 0], relay_down.at[r], relay_send, relay_sem.at[r, 0], (up, e)).start()
        remote(grads.at[far, r, 1], relay_up.at[r], relay_send, relay_sem.at[r, 1], (down, e)).start()

    def raw(r):
        remote(grads.at[up, r, 1], in_down.at[r, 1], raw_send, in_sem.at[r, 0], (up, e)).start()
        remote(grads.at[down, r, 0], in_up.at[r, 0], raw_send, in_sem.at[r, 1], (down, e)).start()

    def combine(r):
        for side, (near, relayed) in enumerate(((near_up, relay_down), (near_down, relay_up))):
            drain(relayed.at[r], relay_sem.at[r, side])

            def add(i, _, near=near, relayed=relayed):
                near[r, i] = (near[r, i].astype(jnp.float32) + relayed[r, i].astype(jnp.float32)).astype(jnp.bfloat16)
                return 0

            lax.fori_loop(0, HALF, add, 0, unroll=True)
            if side == 0:
                remote(near_up.at[r], in_down.at[r, 0], sum_send, in_sem.at[r, 0], (up, e)).start()
            else:
                remote(near_down.at[r], in_up.at[r, 1], sum_send, in_sem.at[r, 1], (down, e)).start()

    row = e * ROWS + lax.broadcasted_iota(jnp.int32, (ROWS, KV_OUT), 0)
    column = lax.broadcasted_iota(jnp.int32, (ROWS, KV_OUT), 1)
    query_live = jnp.where(column < Q_OUT, 1.0, 0.0)
    value_live = jnp.where(row < KV_IN, 1.0, 0.0)

    def home(r):
        drain(in_down.at[r], in_sem.at[r, 0])
        drain(in_up.at[r], in_sem.at[r, 1])
        for half in range(2):

            def one(i, _, half=half):
                slot = r * PER + half * HALF + i
                query = (1 - ids_ref[slot] % 2).astype(jnp.float32)
                live = value_live + query * (query_live - value_live)
                total = own[r, half, i].astype(jnp.float32) + (
                    in_down[r, half, i].astype(jnp.float32) + in_up[r, half, i].astype(jnp.float32)
                )
                gradient = live * total
                state = (live * (beta_coef * held[slot].astype(jnp.float32) + gradient)).astype(jnp.bfloat16)
                fresh[slot] = state
                nest[slot] = (gradient + beta_coef * state.astype(jnp.float32)).astype(jnp.bfloat16)
                return 0

            lax.fori_loop(0, HALF, one, 0, unroll=True)

    def go(r):
        owner = r % 4
        source = nest.at[pl.ds(r * PER, PER)]

        def route(k):
            to_z = (z + k % Z) % Z
            to_half = (x // 2 + k // Z) % 2
            target = 2 * (X * to_z + 2 * to_half + (owner // 2 + to_z) % 2) + owner % 2
            return source.at[2 * to_z + to_half], target

        def send(k, _):
            slab, target = route(k)
            remote(slab, owned.at[r // 4, e], go_send, go_sem.at[r // 4], (d, target)).start()
            return 0

        lax.fori_loop(1, PER, send, 0)

        @pl.when(owner == family)
        def _():
            pltpu.make_async_copy(source.at[place], owned.at[r // 4, e], go_sem.at[r // 4]).start()

        @pl.when(owner != family)
        def _():
            send(0, 0)

    def orthogonalize(r):
        j = r // 4
        query = (1 - ids_ref[r * PER + place] % 2).astype(jnp.float32)
        width = VALUE_SCALE + query * (QUERY_SCALE - VALUE_SCALE)
        drain(owned.at[j], go_sem.at[j])
        block = owned[j].astype(jnp.float32)
        rows = block.reshape(Q_IN, KV_OUT).astype(jnp.bfloat16)
        gram0 = lax.dot_general(rows, rows, (((0,), (0,)), ((), ())), preferred_element_type=jnp.float32)
        factor = polar_factor(gram0) * (width * step_rate)
        high, low = split(factor)
        result = dot(rows, high) + dot(rows, low)
        back[j] = result.reshape(2 * X * Z, ROWS, KV_OUT).astype(jnp.bfloat16)

    def give(j, first, last):
        slot = (4 * j + family) * PER + place

        def send(k, _):
            target = 2 * X * ((z + k % Z) % Z) + (inner + k // Z) % (2 * X)
            remote(back.at[j, target], update.at[slot], back_send, back_sem, (d, target)).start()
            return 0

        lax.fori_loop(first, last, send, 0)

    def given(t, start):
        paced = jnp.minimum(jnp.maximum(1 + (t - start + 1) * PACE, 1), 2 * X * Z)
        return jnp.where(t < ROUNDS, paced, jnp.where(t < start, 1, 2 * X * Z))

    def finish(t):
        r = t - LAG

        @pl.when(r % 4 == family)
        def _():
            orthogonalize(r)
            pltpu.make_async_copy(back.at[r // 4, e], update.at[r * PER + place], back_sem).start()

        for j in range(2):
            start = LAG + 4 * j + family
            give(j, given(t - 1, start), given(t, start))

    relay(0)
    relay(1)
    raw(0)
    load_logit.wait()
    for k in range(1, 2 * X):
        remote(logit, peak_row.at[inner], peak_send.at[0], peak_sem.at[0], (d, row_peer(k))).start()
    pltpu.make_async_copy(logit, peak_row.at[inner], peak_sem.at[0]).start()
    for load in loads:
        load.wait()
    angle = jnp.full((1, KV_OUT), step_ref[0], jnp.int32).astype(jnp.float32) * (math.pi / plan_span)
    step_rate = 0.1 + 0.45 * (1.0 + jnp.cos(angle))
    combine(0)
    raw(1)
    relay(2)
    drain(peak_row, peak_sem.at[0])
    peak_a[...] = jnp.max(peak_row[...], axis=0)
    for k in range(1, Z):
        remote(peak_a, peak_col.at[z], peak_send.at[1], peak_sem.at[1], (d, column_peer(k))).start()
    pltpu.make_async_copy(peak_a, peak_col.at[z], peak_sem.at[1]).start()

    for t in range(LAG):
        combine(t + 1)
        raw(t + 2)
        relay(t + 3)
        home(t)
        if t == 0:
            drain(peak_col, peak_sem.at[1])
            peak_b[...] = jnp.max(peak_col[...], axis=0)
            for other in (up, down, far):
                remote(peak_b, peak_dp.at[d], peak_send.at[2], peak_sem.at[2], (other, e)).start()
            pltpu.make_async_copy(peak_b, peak_dp.at[d], peak_sem.at[2]).start()
        go(t)

    def step(t, _):
        @pl.when(t + 1 < ROUNDS)
        def _():
            combine(t + 1)

        @pl.when(t + 2 < ROUNDS)
        def _():
            raw(t + 2)

        @pl.when(t + 3 < ROUNDS)
        def _():
            relay(t + 3)

        @pl.when(t < ROUNDS)
        def _():
            home(t)
            go(t)

        finish(t)
        return 0

    lax.fori_loop(LAG, ROUNDS + LAG, step, 0)

    drain(peak_dp, peak_sem.at[2])
    peaks_out[...] = jnp.max(peak_dp[...], axis=0)
    drain(peak_row.at[pl.ds(0, 2 * X - 1)], peak_send.at[0])
    drain(peak_col.at[pl.ds(0, Z - 1)], peak_send.at[1])
    drain(peak_dp.at[pl.ds(0, DP - 1)], peak_send.at[2])
    for sem in (relay_send, raw_send, sum_send):
        drain(nest, sem)
    drain(nest.at[pl.ds(0, SLOTS - 2)], go_send)
    drain(nest.at[pl.ds(0, SLOTS - 2)], back_send)
    drain(update, back_sem)


def fused_step(ids, step, grads, momentum, logit):
    slab = (ROWS, KV_OUT)
    bf16 = jnp.bfloat16
    halves = pltpu.VMEM((ROUNDS, HALF) + slab, bf16)
    wholes = pltpu.VMEM((ROUNDS, 2, HALF) + slab, bf16)
    slots = pltpu.VMEM((SLOTS,) + slab, bf16)
    pair = pltpu.VMEM((2, 2 * X * Z) + slab, bf16)
    heads = logit.shape
    dma = pltpu.SemaphoreType.DMA
    vmem = pl.BlockSpec(memory_space=pltpu.VMEM)
    hbm = pl.BlockSpec(memory_space=pltpu.HBM)
    return pl.pallas_call(
        step_kernel,
        in_specs=[hbm, pl.BlockSpec(memory_space=pltpu.SMEM), hbm, hbm, hbm],
        out_specs=[vmem, vmem, vmem],
        out_shape=[
            pltpu.VMEM((SLOTS,) + slab, bf16),
            pltpu.VMEM((SLOTS,) + slab, bf16),
            pltpu.VMEM(heads, jnp.float32),
        ],
        scratch_shapes=[
            pltpu.SMEM(ids.shape, jnp.int32),
            pltpu.VMEM(heads, jnp.float32),
            wholes, halves, halves, slots, halves, halves, wholes, wholes, slots, pair, pair,
            pltpu.VMEM((2 * X,) + heads, jnp.float32),
            pltpu.VMEM((Z,) + heads, jnp.float32),
            pltpu.VMEM((DP,) + heads, jnp.float32),
            pltpu.VMEM(heads, jnp.float32),
            pltpu.VMEM(heads, jnp.float32),
            dma((6,)), dma, dma((ROUNDS, 2)), dma, dma, dma((ROUNDS, 2)), dma, dma((2,)), dma, dma,
            dma((3,)), dma((3,)),
        ],
        compiler_params=pltpu.CompilerParams(
            collective_id=0, has_side_effects=True, vmem_limit_bytes=40 * 2**20
        ),
    )(ids, step, grads, momentum, logit)


def tail_kernel(ids_ref, peaks_ref, fresh, update, fresh_out, update_out, clip_ref, sems):
    copies = [
        pltpu.make_async_copy(fresh, fresh_out, sems.at[0]),
        pltpu.make_async_copy(update, update_out, sems.at[1]),
    ]
    for copy in copies:
        copy.start()
    eta = jnp.minimum(1.0, clip_tau / peaks_ref[...])
    ids = jnp.transpose(jnp.broadcast_to(ids_ref[...], (SLOTS, SLOTS)))[:, 0:1]
    kind = ids % 2
    layer = ids // (2 * eta.shape[1])
    head = (ids // 2) % eta.shape[1]
    lanes = lax.broadcasted_iota(jnp.int32, (SLOTS, eta.shape[1]), 1)
    picked = jnp.zeros((SLOTS, eta.shape[1]), jnp.float32)
    for level in range(eta.shape[0]):
        picked = jnp.where(layer == level, eta[level : level + 1, :], picked)
    slot_eta = jnp.sum(jnp.where(lanes == head, picked, 0.0), axis=1, keepdims=True)
    column = lax.broadcasted_iota(jnp.int32, (SLOTS, KV_OUT), 1)
    rest = jnp.where(kind == 0, jnp.where(column < Q_OUT, slot_eta, 0.0), 1.0)
    clip_ref[...] = jnp.where(column < NOPE_DIM, jnp.sqrt(slot_eta), rest)
    for copy in copies:
        copy.wait()


def write_out(ids, peaks, fresh, update):
    vmem = pl.BlockSpec(memory_space=pltpu.VMEM)
    anywhere = pl.BlockSpec(memory_space=pl.ANY)
    return pl.pallas_call(
        tail_kernel,
        in_specs=[vmem, vmem, vmem, vmem],
        out_specs=[anywhere, anywhere, vmem],
        out_shape=[
            jax.ShapeDtypeStruct(fresh.shape, fresh.dtype),
            jax.ShapeDtypeStruct(update.shape, update.dtype),
            jax.ShapeDtypeStruct((SLOTS, KV_OUT), jnp.float32),
        ],
        scratch_shapes=[pltpu.SemaphoreType.DMA((2,))],
    )(ids, peaks, fresh, update)


def body(grad_parts, momentum, block_ids, step, logit_max):
    grads = grad_parts.reshape(DP, ROUNDS, 2, HALF, ROWS, KV_OUT)
    ids, grads, momentum, logit = (
        pltpu.with_memory_space_constraint(a, pltpu.HBM) for a in (block_ids, grads, momentum, logit_max[0, 0])
    )
    results = fused_step(ids, step, grads, momentum, logit)
    fresh, update, peaks = (pltpu.with_memory_space_constraint(a, pltpu.VMEM) for a in results)
    return tuple(write_out(block_ids.reshape(1, SLOTS), peaks, fresh, update))


def solution(mesh):
    in_specs = (
        P("dp", None, "expert", None),
        P("dp", "expert", None),
        P("dp"),
        P(),
        P("dp", "expert", None, None),
    )
    out_specs = (P("dp", "expert", None), P("dp", "expert", None), P("dp", None))
    return jax.shard_map(body, mesh=mesh, in_specs=in_specs, out_specs=out_specs, check_vma=False)
```

```python
import math

import jax
import jax.numpy as jnp
from jax import lax
from jax.experimental import pallas as pl
from jax.experimental.pallas import tpu as pltpu
from jax.sharding import PartitionSpec as P

Q_IN = 1536
KV_IN = 512
NOPE_DIM = 128
NS_STEPS = 5
Q_OUT = 192
KV_OUT = 256
ROWS = 24
SLOTS = 128
ROUNDS = 8
PER = 16
HALF = 8
LAG = 2
PACE = 16
Z = 8
X = 4
DP = 4
FULL = -(-KV_IN // ROWS)
ALL = 6
FEW = 5
ARRIVING = FULL * ALL + (2 * X * Z - FULL) * FEW
MESH = pl.DeviceIdType.MESH

quintic_a = 3.4445
quintic_b = -4.775
quintic_c = 2.0315
norm_eps = 1e-07
beta_coef = 0.95
clip_tau = 100.0
plan_span = 10000.0
rms_match = 0.2
QUERY_SCALE = rms_match * math.sqrt(max(Q_IN, Q_OUT))
VALUE_SCALE = rms_match * math.sqrt(max(KV_IN, KV_OUT))


def split(value):
    high = value.astype(jnp.bfloat16)
    low = (value - high.astype(jnp.float32)).astype(jnp.bfloat16)
    return high, low


def dot(left, right):
    return jnp.dot(left, right, preferred_element_type=jnp.float32)


def product(left, right):
    (lh, ll), (rh, rl) = left, right
    return dot(lh, rh) + (dot(lh, rl) + dot(ll, rh))


def polar_factor(gram0):
    rows = lax.broadcasted_iota(jnp.int32, gram0.shape, 0)
    columns = lax.broadcasted_iota(jnp.int32, gram0.shape, 1)
    eye = jnp.where(rows == columns, 1.0, 0.0)
    squares = jnp.sum(jnp.sum(gram0 * eye, axis=1, keepdims=True), axis=0, keepdims=True)
    inverse = 1.0 / (jnp.sqrt(squares) + norm_eps)
    gram = (gram0 * inverse) * inverse
    factor = None
    for sweep in range(NS_STEPS):
        parts = split(gram)
        poly = quintic_a * eye + quintic_b * gram + quintic_c * product(parts, parts)
        poly_parts = split(poly)
        factor = poly if factor is None else product(split(factor), poly_parts)
        if sweep < NS_STEPS - 1:
            gram = product(split(product(parts, poly_parts)), poly_parts)
    return factor * inverse


def drain(ref, sem):
    pltpu.make_async_copy(ref, ref, sem).wait()


def step_kernel(
    ids_hbm, step_ref, grads, momentum, logit_hbm, fresh, update, peaks_out,
    ids_ref, logit,
    own, near_up, near_down, held, relay_up, relay_down, in_up, in_down, nest, owned, back, returned,
    peak_row, peak_col, peak_dp, peak_a, peak_b,
    load_sem, relay_send, relay_sem, raw_send, sum_send, in_sem, go_send, go_sem, back_send, back_sem,
    peak_send, peak_sem,
):
    d = lax.axis_index("dp")
    e = lax.axis_index("expert")
    z, x, core = e // (2 * X), (e // 2) % X, e % 2
    inner = e % (2 * X)
    family = 2 * ((x + z) % 2) + core
    place = 2 * z + x // 2
    up, down, far = (d + 1) % DP, (d + 3) % DP, (d + 2) % DP

    def remote(source, target, send, recv, where):
        return pltpu.make_async_remote_copy(
            src_ref=source, dst_ref=target, send_sem=send, recv_sem=recv, device_id=where, device_id_type=MESH
        )

    def row_peer(k):
        return 2 * X * z + (inner + k) % (2 * X)

    def column_peer(k):
        return 2 * X * ((z + k) % Z) + inner

    barrier = pltpu.get_barrier_semaphore()

    def greet(where):
        pl.semaphore_signal(barrier, inc=1, device_id=where, device_id_type=MESH)

    for other in (up, down, far):
        greet((other, e))
    for k in range(1, 2 * X):
        greet((d, row_peer(k)))
    for k in range(1, Z):
        greet((d, column_peer(k)))
    loads = [
        pltpu.make_async_copy(grads.at[up, :, 0], near_up, load_sem.at[0]),
        pltpu.make_async_copy(grads.at[down, :, 1], near_down, load_sem.at[1]),
        pltpu.make_async_copy(grads.at[d], own, load_sem.at[2]),
        pltpu.make_async_copy(momentum, held, load_sem.at[3]),
        pltpu.make_async_copy(ids_hbm, ids_ref, load_sem.at[4]),
    ]
    load_logit = pltpu.make_async_copy(logit_hbm, logit, load_sem.at[5])
    load_logit.start()
    for load in loads:
        load.start()
    pl.semaphore_wait(barrier, DP - 1 + 2 * X - 1 + Z - 1)

    def relay(r):
        remote(grads.at[far, r, 0], relay_down.at[r], relay_send, relay_sem.at[r, 0], (up, e)).start()
        remote(grads.at[far, r, 1], relay_up.at[r], relay_send, relay_sem.at[r, 1], (down, e)).start()

    def raw(r):
        remote(grads.at[up, r, 1], in_down.at[r, 1], raw_send, in_sem.at[r, 0], (up, e)).start()
        remote(grads.at[down, r, 0], in_up.at[r, 0], raw_send, in_sem.at[r, 1], (down, e)).start()

    def combine(r):
        for side, (near, relayed) in enumerate(((near_up, relay_down), (near_down, relay_up))):
            drain(relayed.at[r], relay_sem.at[r, side])

            def add(i, _, near=near, relayed=relayed):
                near[r, i] = (near[r, i].astype(jnp.float32) + relayed[r, i].astype(jnp.float32)).astype(jnp.bfloat16)
                return 0

            lax.fori_loop(0, HALF, add, 0, unroll=True)
            if side == 0:
                remote(near_up.at[r], in_down.at[r, 0], sum_send, in_sem.at[r, 0], (up, e)).start()
            else:
                remote(near_down.at[r], in_up.at[r, 1], sum_send, in_sem.at[r, 1], (down, e)).start()

    row = e * ROWS + lax.broadcasted_iota(jnp.int32, (ROWS, KV_OUT), 0)
    column = lax.broadcasted_iota(jnp.int32, (ROWS, KV_OUT), 1)
    query_live = jnp.where(column < Q_OUT, 1.0, 0.0)
    value_live = jnp.where(row < KV_IN, 1.0, 0.0)
    lane = lax.broadcasted_iota(jnp.int32, (8, 128), 1)
    wide = e < FULL
    wide_tile = 0 * lane + e < FULL

    def by_width(act):
        @pl.when(wide)
        def _():
            act(ALL)

        @pl.when(jnp.logical_not(wide))
        def _():
            act(FEW)


    def home(r):
        drain(in_down.at[r], in_sem.at[r, 0])
        drain(in_up.at[r], in_sem.at[r, 1])
        for half in range(2):

            def one(i, _, half=half):
                slot = r * PER + half * HALF + i
                query = (1 - ids_ref[slot] % 2).astype(jnp.float32)
                live = value_live + query * (query_live - value_live)
                total = own[r, half, i].astype(jnp.float32) + (
                    in_down[r, half, i].astype(jnp.float32) + in_up[r, half, i].astype(jnp.float32)
                )
                gradient = live * total
                state = (live * (beta_coef * held[slot].astype(jnp.float32) + gradient)).astype(jnp.bfloat16)
                fresh[slot] = state
                ahead = gradient + beta_coef * state.astype(jnp.float32)
                left = ahead[:, :128].reshape(3, 8, 128)
                right = ahead[:, 128:].reshape(3, 8, 128)
                folded = jnp.where(wide_tile, right[0], right[0] + pltpu.roll(right[1], 64, 1))
                second = jnp.where(wide_tile, right[1], right[2])
                tiles = jnp.concatenate([left, folded[None], second[None], right[2:3]], axis=0)
                nest[slot] = tiles.astype(jnp.bfloat16)
                return 0

            lax.fori_loop(0, HALF, one, 0, unroll=True)

    def go(r):
        owner = r % 4
        first = (r // 4) * 2 * X * Z * ALL + e * ALL

        def route(k):
            to_z = (z + k % Z) % Z
            to_half = (x // 2 + k // Z) % 2
            target = 2 * (X * to_z + 2 * to_half + (owner // 2 + to_z) % 2) + owner % 2
            return r * PER + 2 * to_z + to_half, target

        def push(count):
            arriving = owned.at[pl.ds(first, count)]

            def send(k, _):
                slot, target = route(k)
                remote(nest.at[slot, pl.ds(0, count)], arriving, go_send, go_sem.at[r // 4], (d, target)).start()
                return 0

            lax.fori_loop(1, PER, send, 0)

            @pl.when(owner == family)
            def _():
                pltpu.make_async_copy(nest.at[r * PER + place, pl.ds(0, count)], arriving, go_sem.at[r // 4]).start()

            @pl.when(owner != family)
            def _():
                send(0, 0)

        by_width(push)

    def orthogonalize(r):
        j = r // 4
        query = (1 - ids_ref[r * PER + place] % 2).astype(jnp.float32)
        width = VALUE_SCALE + query * (QUERY_SCALE - VALUE_SCALE)
        base = j * 2 * X * Z * ALL
        drain(owned.at[pl.ds(base, ARRIVING)], go_sem.at[j])
        tiles = owned[pl.ds(base, 2 * X * Z * ALL)].astype(jnp.float32).reshape(2 * X * Z, ALL, 8, 128)
        half = lax.broadcasted_iota(jnp.int32, (2 * X * Z - FULL, 8, 128), 2) < 64
        folded = tiles[FULL:, 3]
        narrow = [
            jnp.where(half, folded, 0.0),
            jnp.where(half, pltpu.roll(folded, 64, 2), 0.0),
            tiles[FULL:, 4],
        ]
        right = jnp.concatenate([tiles[:FULL, 3:], jnp.stack(narrow, axis=1)], axis=0)
        parts = [tiles[:, :3].reshape(Q_IN, 128), right.reshape(Q_IN, 128)]
        rows = jnp.concatenate(parts, axis=1).astype(jnp.bfloat16)
        gram0 = lax.dot_general(rows, rows, (((0,), (0,)), ((), ())), preferred_element_type=jnp.float32)
        factor = polar_factor(gram0) * (width * step_rate)
        high, low = split(factor)
        result = dot(rows, high) + dot(rows, low)
        left = result[:, :128].reshape(2 * X * Z, 3, 8, 128)
        right = result[:, 128:].reshape(2 * X * Z, 3, 8, 128)
        narrow = right[FULL:]
        folded = jnp.where(half, narrow[:, 0], pltpu.roll(narrow[:, 1], 64, 2))
        packed = jnp.stack([folded, narrow[:, 2], narrow[:, 2]], axis=1)
        tiles = jnp.concatenate([left, jnp.concatenate([right[:FULL], packed], axis=0)], axis=1)
        back[pl.ds(base, 2 * X * Z * ALL)] = tiles.reshape(2 * X * Z * ALL, 8, 128).astype(jnp.bfloat16)

    def give(j, first, last):
        slot = (4 * j + family) * PER + place

        def send(k, _):
            target = 2 * X * ((z + k % Z) % Z) + (inner + k // Z) % (2 * X)

            def push(count):
                remote(
                    back.at[pl.ds((j * 2 * X * Z + target) * ALL, count)], returned.at[slot, pl.ds(0, count)],
                    back_send, back_sem.at[4 * j + family], (d, target),
                ).start()

            @pl.when(target < FULL)
            def _():
                push(ALL)

            @pl.when(target >= FULL)
            def _():
                push(FEW)

            return 0

        lax.fori_loop(first, last, send, 0)

    def keep(r):
        def move(count):
            pltpu.make_async_copy(
                back.at[pl.ds(((r // 4) * 2 * X * Z + e) * ALL, count)],
                returned.at[r * PER + place, pl.ds(0, count)],
                back_sem.at[r],
            ).start()

        by_width(move)

    def unpack(r):
        drain_rows = pl.ds(r * PER, PER)

        @pl.when(wide)
        def _():
            drain(returned.at[drain_rows], back_sem.at[r])

            def one(i, _):
                tiles = returned[r * PER + i].astype(jnp.float32)
                update[r * PER + i] = jnp.concatenate(
                    [tiles[:3].reshape(ROWS, 128), tiles[3:].reshape(ROWS, 128)], axis=1
                ).astype(jnp.bfloat16)
                return 0

            lax.fori_loop(0, PER, one, 0, unroll=4)

        @pl.when(jnp.logical_not(wide))
        def _():
            drain(returned.at[drain_rows, pl.ds(0, FEW)], back_sem.at[r])

            def one(i, _):
                tiles = returned[r * PER + i, pl.ds(0, FEW)].astype(jnp.float32)
                first = jnp.where(lane < 64, tiles[3], 0.0)
                second = jnp.where(lane < 64, pltpu.roll(tiles[3], 64, 1), 0.0)
                right = jnp.concatenate([first, second, tiles[4]], axis=0)
                update[r * PER + i] = jnp.concatenate(
                    [tiles[:3].reshape(ROWS, 128), right], axis=1
                ).astype(jnp.bfloat16)
                return 0

            lax.fori_loop(0, PER, one, 0, unroll=4)

    def given(t, start):
        paced = jnp.minimum(jnp.maximum(1 + (t - start + 1) * PACE, 1), 2 * X * Z)
        return jnp.where(t < ROUNDS, paced, jnp.where(t < start, 1, 2 * X * Z))

    def finish(t):
        r = t - LAG

        @pl.when(r % 4 == family)
        def _():
            orthogonalize(r)
            keep(r)

        for j in range(2):
            start = LAG + 4 * j + family
            give(j, given(t - 1, start), given(t, start))

    relay(0)
    raw(0)
    load_logit.wait()
    for k in range(1, 2 * X):
        remote(logit, peak_row.at[inner], peak_send.at[0], peak_sem.at[0], (d, row_peer(k))).start()
    pltpu.make_async_copy(logit, peak_row.at[inner], peak_sem.at[0]).start()
    for load in loads:
        load.wait()
    angle = jnp.full((1, KV_OUT), step_ref[0], jnp.int32).astype(jnp.float32) * (math.pi / plan_span)
    step_rate = 0.1 + 0.45 * (1.0 + jnp.cos(angle))
    combine(0)
    relay(1)
    raw(1)
    relay(2)
    drain(peak_row, peak_sem.at[0])
    peak_a[...] = jnp.max(peak_row[...], axis=0)
    for k in range(1, Z):
        remote(peak_a, peak_col.at[z], peak_send.at[1], peak_sem.at[1], (d, column_peer(k))).start()
    pltpu.make_async_copy(peak_a, peak_col.at[z], peak_sem.at[1]).start()

    for t in range(LAG):
        home(t)
        if t == 0:
            drain(peak_col, peak_sem.at[1])
            peak_b[...] = jnp.max(peak_col[...], axis=0)
            for other in (up, down, far):
                remote(peak_b, peak_dp.at[d], peak_send.at[2], peak_sem.at[2], (other, e)).start()
            pltpu.make_async_copy(peak_b, peak_dp.at[d], peak_sem.at[2]).start()
        go(t)
        combine(t + 1)
        raw(t + 2)
        relay(t + 3)

    def step(t, _):
        @pl.when(t < ROUNDS)
        def _():
            home(t)
            go(t)

        @pl.when(t + 1 < ROUNDS)
        def _():
            combine(t + 1)

        @pl.when(t + 2 < ROUNDS)
        def _():
            raw(t + 2)

        @pl.when(t + 3 < ROUNDS)
        def _():
            relay(t + 3)

        finish(t)
        return 0

    lax.fori_loop(LAG, ROUNDS + LAG, step, 0)

    def collect(r, _):
        unpack(r)
        return 0

    lax.fori_loop(0, ROUNDS, collect, 0)
    drain(peak_dp, peak_sem.at[2])
    peaks_out[...] = jnp.max(peak_dp[...], axis=0)
    drain(peak_row.at[pl.ds(0, 2 * X - 1)], peak_send.at[0])
    drain(peak_col.at[pl.ds(0, Z - 1)], peak_send.at[1])
    drain(peak_dp.at[pl.ds(0, DP - 1)], peak_send.at[2])
    for sem in (relay_send, raw_send, sum_send):
        drain(held, sem)

    def settle(count):
        drain(nest.at[pl.ds(0, (SLOTS - 2) * count // ALL)], go_send)
        drain(back.at[pl.ds(0, 2 * (ARRIVING - count))], back_send)

    by_width(settle)


def fused_step(ids, step, grads, momentum, logit):
    slab = (ROWS, KV_OUT)
    bf16 = jnp.bfloat16
    halves = pltpu.VMEM((ROUNDS, HALF) + slab, bf16)
    wholes = pltpu.VMEM((ROUNDS, 2, HALF) + slab, bf16)
    slots = pltpu.VMEM((SLOTS,) + slab, bf16)
    tiles = pltpu.VMEM((SLOTS, ALL, 8, 128), bf16)
    flat = pltpu.VMEM((SLOTS * ALL, 8, 128), bf16)
    heads = logit.shape
    dma = pltpu.SemaphoreType.DMA
    vmem = pl.BlockSpec(memory_space=pltpu.VMEM)
    hbm = pl.BlockSpec(memory_space=pltpu.HBM)
    return pl.pallas_call(
        step_kernel,
        in_specs=[hbm, pl.BlockSpec(memory_space=pltpu.SMEM), hbm, hbm, hbm],
        out_specs=[vmem, vmem, vmem],
        out_shape=[
            pltpu.VMEM((SLOTS,) + slab, bf16),
            pltpu.VMEM((SLOTS,) + slab, bf16),
            pltpu.VMEM(heads, jnp.float32),
        ],
        scratch_shapes=[
            pltpu.SMEM(ids.shape, jnp.int32),
            pltpu.VMEM(heads, jnp.float32),
            wholes, halves, halves, slots, halves, halves, wholes, wholes, tiles, flat, flat, tiles,
            pltpu.VMEM((2 * X,) + heads, jnp.float32),
            pltpu.VMEM((Z,) + heads, jnp.float32),
            pltpu.VMEM((DP,) + heads, jnp.float32),
            pltpu.VMEM(heads, jnp.float32),
            pltpu.VMEM(heads, jnp.float32),
            dma((6,)), dma, dma((ROUNDS, 2)), dma, dma, dma((ROUNDS, 2)), dma, dma((2,)), dma, dma((ROUNDS,)),
            dma((3,)), dma((3,)),
        ],
        compiler_params=pltpu.CompilerParams(
            collective_id=0, has_side_effects=True, vmem_limit_bytes=40 * 2**20
        ),
    )(ids, step, grads, momentum, logit)


def tail_kernel(ids_ref, peaks_ref, fresh, update, fresh_out, update_out, clip_ref, sems):
    copies = [
        pltpu.make_async_copy(fresh, fresh_out, sems.at[0]),
        pltpu.make_async_copy(update, update_out, sems.at[1]),
    ]
    for copy in copies:
        copy.start()
    eta = jnp.minimum(1.0, clip_tau / peaks_ref[...])
    ids = jnp.transpose(jnp.broadcast_to(ids_ref[...], (SLOTS, SLOTS)))[:, 0:1]
    kind = ids % 2
    layer = ids // (2 * eta.shape[1])
    head = (ids // 2) % eta.shape[1]
    lanes = lax.broadcasted_iota(jnp.int32, (SLOTS, eta.shape[1]), 1)
    picked = jnp.zeros((SLOTS, eta.shape[1]), jnp.float32)
    for level in range(eta.shape[0]):
        picked = jnp.where(layer == level, eta[level : level + 1, :], picked)
    slot_eta = jnp.sum(jnp.where(lanes == head, picked, 0.0), axis=1, keepdims=True)
    column = lax.broadcasted_iota(jnp.int32, (SLOTS, KV_OUT), 1)
    rest = jnp.where(kind == 0, jnp.where(column < Q_OUT, slot_eta, 0.0), 1.0)
    clip_ref[...] = jnp.where(column < NOPE_DIM, jnp.sqrt(slot_eta), rest)
    for copy in copies:
        copy.wait()


def write_out(ids, peaks, fresh, update):
    vmem = pl.BlockSpec(memory_space=pltpu.VMEM)
    anywhere = pl.BlockSpec(memory_space=pl.ANY)
    return pl.pallas_call(
        tail_kernel,
        in_specs=[vmem, vmem, vmem, vmem],
        out_specs=[anywhere, anywhere, vmem],
        out_shape=[
            jax.ShapeDtypeStruct(fresh.shape, fresh.dtype),
            jax.ShapeDtypeStruct(update.shape, update.dtype),
            jax.ShapeDtypeStruct((SLOTS, KV_OUT), jnp.float32),
        ],
        scratch_shapes=[pltpu.SemaphoreType.DMA((2,))],
    )(ids, peaks, fresh, update)


def body(grad_parts, momentum, block_ids, step, logit_max):
    grads = grad_parts.reshape(DP, ROUNDS, 2, HALF, ROWS, KV_OUT)
    ids, grads, momentum, logit = (
        pltpu.with_memory_space_constraint(a, pltpu.HBM) for a in (block_ids, grads, momentum, logit_max[0, 0])
    )
    results = fused_step(ids, step, grads, momentum, logit)
    fresh, update, peaks = (pltpu.with_memory_space_constraint(a, pltpu.VMEM) for a in results)
    return tuple(write_out(block_ids.reshape(1, SLOTS), peaks, fresh, update))


def solution(mesh):
    in_specs = (
        P("dp", None, "expert", None),
        P("dp", "expert", None),
        P("dp"),
        P(),
        P("dp", "expert", None, None),
    )
    out_specs = (P("dp", "expert", None), P("dp", "expert", None), P("dp", None))
    return jax.shard_map(body, mesh=mesh, in_specs=in_specs, out_specs=out_specs, check_vma=False)
```

```python
import math

import jax
import jax.numpy as jnp
from jax import lax
from jax.experimental import pallas as pl
from jax.experimental.pallas import tpu as pltpu
from jax.sharding import PartitionSpec as P

Q_IN = 1536
KV_IN = 512
NOPE_DIM = 128
NS_STEPS = 5
Q_OUT = 192
KV_OUT = 256
ROWS = 24
SLOTS = 128
ROUNDS = 8
PER = 16
HALF = 8
LAG = 2
PACE = 16
Z = 8
X = 4
DP = 4
FULL = -(-KV_IN // ROWS)
ALL = 6
FEW = 5
ARRIVING = FULL * ALL + (2 * X * Z - FULL) * FEW
MESH = pl.DeviceIdType.MESH

quintic_a = 3.4445
quintic_b = -4.775
quintic_c = 2.0315
norm_eps = 1e-07
beta_coef = 0.95
clip_tau = 100.0
plan_span = 10000.0
rms_match = 0.2
QUERY_SCALE = rms_match * math.sqrt(max(Q_IN, Q_OUT))
VALUE_SCALE = rms_match * math.sqrt(max(KV_IN, KV_OUT))


def split(value):
    high = value.astype(jnp.bfloat16)
    low = (value - high.astype(jnp.float32)).astype(jnp.bfloat16)
    return high, low


def dot(left, right):
    return jnp.dot(left, right, preferred_element_type=jnp.float32)


def product(left, right):
    (lh, ll), (rh, rl) = left, right
    return dot(lh, rh) + (dot(lh, rl) + dot(ll, rh))


def polar_factor(gram0):
    rows = lax.broadcasted_iota(jnp.int32, gram0.shape, 0)
    columns = lax.broadcasted_iota(jnp.int32, gram0.shape, 1)
    eye = jnp.where(rows == columns, 1.0, 0.0)
    squares = jnp.sum(jnp.sum(gram0 * eye, axis=1, keepdims=True), axis=0, keepdims=True)
    inverse = 1.0 / (jnp.sqrt(squares) + norm_eps)
    gram = (gram0 * inverse) * inverse
    factor = None
    for sweep in range(NS_STEPS):
        parts = split(gram)
        poly = quintic_a * eye + quintic_b * gram + quintic_c * product(parts, parts)
        poly_parts = split(poly)
        factor = poly if factor is None else product(split(factor), poly_parts)
        if sweep < NS_STEPS - 1:
            gram = product(split(product(parts, poly_parts)), poly_parts)
    return factor * inverse


def drain(ref, sem):
    pltpu.make_async_copy(ref, ref, sem).wait()


def step_kernel(
    ids_hbm, ids_row, step_ref, grads, momentum, logit_hbm, fresh, update, clip_ref,
    ids_ref, ids_lane, logit,
    own, near_up, near_down, held, relay_up, relay_down, in_up, in_down, nest, owned, back, returned,
    peak_row, peak_col, peak_dp, peak_a, peak_b,
    load_sem, relay_send, relay_sem, raw_send, sum_send, in_sem, go_send, go_sem, back_send, back_sem,
    peak_send, peak_sem,
):
    d = lax.axis_index("dp")
    e = lax.axis_index("expert")
    z, x, core = e // (2 * X), (e // 2) % X, e % 2
    inner = e % (2 * X)
    family = (x + z) % 2 + 2 * core
    place = 2 * z + x // 2
    up, down, far = (d + 1) % DP, (d + 3) % DP, (d + 2) % DP

    def remote(source, target, send, recv, where):
        return pltpu.make_async_remote_copy(
            src_ref=source, dst_ref=target, send_sem=send, recv_sem=recv, device_id=where, device_id_type=MESH
        )

    def row_peer(k):
        return 2 * X * z + (inner + k) % (2 * X)

    def column_peer(k):
        return 2 * X * ((z + k) % Z) + inner

    barrier = pltpu.get_barrier_semaphore()

    def greet(where):
        pl.semaphore_signal(barrier, inc=1, device_id=where, device_id_type=MESH)

    for other in (up, down, far):
        greet((other, e))
    for k in range(1, 2 * X):
        greet((d, row_peer(k)))
    for k in range(1, Z):
        greet((d, column_peer(k)))
    loads = [
        pltpu.make_async_copy(grads.at[up, :, 0], near_up, load_sem.at[0]),
        pltpu.make_async_copy(grads.at[down, :, 1], near_down, load_sem.at[1]),
        pltpu.make_async_copy(grads.at[d], own, load_sem.at[2]),
        pltpu.make_async_copy(momentum, held, load_sem.at[3]),
        pltpu.make_async_copy(ids_hbm, ids_ref, load_sem.at[4]),
        pltpu.make_async_copy(ids_row, ids_lane, load_sem.at[6]),
    ]
    load_logit = pltpu.make_async_copy(logit_hbm, logit, load_sem.at[5])
    load_logit.start()
    for load in loads:
        load.start()
    pl.semaphore_wait(barrier, DP - 1 + 2 * X - 1 + Z - 1)

    def relay(r):
        remote(grads.at[far, r, 0], relay_down.at[r], relay_send, relay_sem.at[r, 0], (up, e)).start()
        remote(grads.at[far, r, 1], relay_up.at[r], relay_send, relay_sem.at[r, 1], (down, e)).start()

    def raw(r):
        remote(grads.at[up, r, 1], in_down.at[r, 1], raw_send, in_sem.at[r, 0], (up, e)).start()
        remote(grads.at[down, r, 0], in_up.at[r, 0], raw_send, in_sem.at[r, 1], (down, e)).start()

    def combine(r):
        for side, (near, relayed) in enumerate(((near_up, relay_down), (near_down, relay_up))):
            drain(relayed.at[r], relay_sem.at[r, side])

            def add(i, _, near=near, relayed=relayed):
                near[r, i] = (near[r, i].astype(jnp.float32) + relayed[r, i].astype(jnp.float32)).astype(jnp.bfloat16)
                return 0

            lax.fori_loop(0, HALF, add, 0, unroll=True)
            if side == 0:
                remote(near_up.at[r], in_down.at[r, 0], sum_send, in_sem.at[r, 0], (up, e)).start()
            else:
                remote(near_down.at[r], in_up.at[r, 1], sum_send, in_sem.at[r, 1], (down, e)).start()

    row = e * ROWS + lax.broadcasted_iota(jnp.int32, (ROWS, KV_OUT), 0)
    column = lax.broadcasted_iota(jnp.int32, (ROWS, KV_OUT), 1)
    query_live = jnp.where(column < Q_OUT, 1.0, 0.0)
    value_live = jnp.where(row < KV_IN, 1.0, 0.0)
    lane = lax.broadcasted_iota(jnp.int32, (8, 128), 1)
    wide = e < FULL
    wide_tile = 0 * lane + e < FULL

    def by_width(act):
        @pl.when(wide)
        def _():
            act(ALL)

        @pl.when(jnp.logical_not(wide))
        def _():
            act(FEW)


    def home(r):
        drain(in_down.at[r], in_sem.at[r, 0])
        drain(in_up.at[r], in_sem.at[r, 1])
        for half in range(2):

            def one(i, _, half=half):
                slot = r * PER + half * HALF + i
                query = (1 - ids_ref[slot] % 2).astype(jnp.float32)
                live = value_live + query * (query_live - value_live)
                total = own[r, half, i].astype(jnp.float32) + (
                    in_down[r, half, i].astype(jnp.float32) + in_up[r, half, i].astype(jnp.float32)
                )
                gradient = live * total
                state = (live * (beta_coef * held[slot].astype(jnp.float32) + gradient)).astype(jnp.bfloat16)
                fresh[slot] = state
                ahead = gradient + beta_coef * state.astype(jnp.float32)
                left = ahead[:, :128].reshape(3, 8, 128)
                right = ahead[:, 128:].reshape(3, 8, 128)
                folded = jnp.where(wide_tile, right[0], right[0] + pltpu.roll(right[1], 64, 1))
                second = jnp.where(wide_tile, right[1], right[2])
                tiles = jnp.concatenate([left, folded[None], second[None], right[2:3]], axis=0)
                nest[slot] = tiles.astype(jnp.bfloat16)
                return 0

            lax.fori_loop(0, HALF, one, 0, unroll=True)

    def go(r, low, high):
        owner = r % 4
        first = (r // 4) * 2 * X * Z * ALL + e * ALL

        def route(k):
            to_z = (z + k % Z) % Z
            to_half = (x // 2 + k // Z) % 2
            target = 2 * (X * to_z + 2 * to_half + (owner + to_z) % 2) + owner // 2
            return r * PER + 2 * to_z + to_half, target

        def push(count):
            arriving = owned.at[pl.ds(first, count)]

            def send(k, _):
                slot, target = route(k)
                remote(nest.at[slot, pl.ds(0, count)], arriving, go_send, go_sem.at[r // 4], (d, target)).start()
                return 0

            lax.fori_loop(max(low, 1), high, send, 0)
            if low > 0:
                return

            @pl.when(owner == family)
            def _():
                pltpu.make_async_copy(nest.at[r * PER + place, pl.ds(0, count)], arriving, go_sem.at[r // 4]).start()

            @pl.when(owner != family)
            def _():
                send(0, 0)

        by_width(push)

    def orthogonalize(r):
        j = r // 4
        query = (1 - ids_ref[r * PER + place] % 2).astype(jnp.float32)
        width = VALUE_SCALE + query * (QUERY_SCALE - VALUE_SCALE)
        base = j * 2 * X * Z * ALL
        drain(owned.at[pl.ds(base, ARRIVING)], go_sem.at[j])
        tiles = owned[pl.ds(base, 2 * X * Z * ALL)].astype(jnp.float32).reshape(2 * X * Z, ALL, 8, 128)
        half = lax.broadcasted_iota(jnp.int32, (2 * X * Z - FULL, 8, 128), 2) < 64
        folded = tiles[FULL:, 3]
        narrow = [
            jnp.where(half, folded, 0.0),
            jnp.where(half, pltpu.roll(folded, 64, 2), 0.0),
            tiles[FULL:, 4],
        ]
        right = jnp.concatenate([tiles[:FULL, 3:], jnp.stack(narrow, axis=1)], axis=0)
        parts = [tiles[:, :3].reshape(Q_IN, 128), right.reshape(Q_IN, 128)]
        rows = jnp.concatenate(parts, axis=1).astype(jnp.bfloat16)
        gram0 = lax.dot_general(rows, rows, (((0,), (0,)), ((), ())), preferred_element_type=jnp.float32)
        factor = polar_factor(gram0) * (width * step_rate)
        high, low = split(factor)
        result = dot(rows, high) + dot(rows, low)
        left = result[:, :128].reshape(2 * X * Z, 3, 8, 128)
        right = result[:, 128:].reshape(2 * X * Z, 3, 8, 128)
        narrow = right[FULL:]
        folded = jnp.where(half, narrow[:, 0], pltpu.roll(narrow[:, 1], 64, 2))
        packed = jnp.stack([folded, narrow[:, 2], narrow[:, 2]], axis=1)
        tiles = jnp.concatenate([left, jnp.concatenate([right[:FULL], packed], axis=0)], axis=1)
        back[pl.ds(base, 2 * X * Z * ALL)] = tiles.reshape(2 * X * Z * ALL, 8, 128).astype(jnp.bfloat16)

    def give(j, first, last):
        slot = (4 * j + family) * PER + place

        def send(k, _):
            target = 2 * X * ((z + k % Z) % Z) + (inner + k // Z) % (2 * X)

            def push(count):
                remote(
                    back.at[pl.ds((j * 2 * X * Z + target) * ALL, count)], returned.at[slot, pl.ds(0, count)],
                    back_send, back_sem.at[4 * j + family], (d, target),
                ).start()

            @pl.when(target < FULL)
            def _():
                push(ALL)

            @pl.when(target >= FULL)
            def _():
                push(FEW)

            return 0

        lax.fori_loop(first, last, send, 0)

    def keep(r):
        def move(count):
            pltpu.make_async_copy(
                back.at[pl.ds(((r // 4) * 2 * X * Z + e) * ALL, count)],
                returned.at[r * PER + place, pl.ds(0, count)],
                back_sem.at[r],
            ).start()

        by_width(move)

    def unpack(r):
        drain_rows = pl.ds(r * PER, PER)

        @pl.when(wide)
        def _():
            drain(returned.at[drain_rows], back_sem.at[r])

            def one(i, _):
                tiles = returned[r * PER + i].astype(jnp.float32)
                update[r * PER + i] = jnp.concatenate(
                    [tiles[:3].reshape(ROWS, 128), tiles[3:].reshape(ROWS, 128)], axis=1
                ).astype(jnp.bfloat16)
                return 0

            lax.fori_loop(0, PER, one, 0, unroll=4)

        @pl.when(jnp.logical_not(wide))
        def _():
            drain(returned.at[drain_rows, pl.ds(0, FEW)], back_sem.at[r])

            def one(i, _):
                tiles = returned[r * PER + i, pl.ds(0, FEW)].astype(jnp.float32)
                first = jnp.where(lane < 64, tiles[3], 0.0)
                second = jnp.where(lane < 64, pltpu.roll(tiles[3], 64, 1), 0.0)
                right = jnp.concatenate([first, second, tiles[4]], axis=0)
                update[r * PER + i] = jnp.concatenate(
                    [tiles[:3].reshape(ROWS, 128), right], axis=1
                ).astype(jnp.bfloat16)
                return 0

            lax.fori_loop(0, PER, one, 0, unroll=4)

    def given(t, start):
        paced = jnp.minimum(jnp.maximum(1 + (t - start + 1) * PACE, 1), 2 * X * Z)
        return jnp.where(t < ROUNDS, paced, jnp.where(t < start, 1, 2 * X * Z))

    def finish(t):
        r = t - LAG

        @pl.when(r % 4 == family)
        def _():
            orthogonalize(r)
            keep(r)

        for j in range(2):
            start = LAG + 4 * j + family
            give(j, given(t - 1, start), given(t, start))

    relay(0)
    raw(0)
    load_logit.wait()
    for k in range(1, 2 * X):
        remote(logit, peak_row.at[inner], peak_send.at[0], peak_sem.at[0], (d, row_peer(k))).start()
    pltpu.make_async_copy(logit, peak_row.at[inner], peak_sem.at[0]).start()
    for load in loads:
        load.wait()
    angle = jnp.full((1, KV_OUT), step_ref[0], jnp.int32).astype(jnp.float32) * (math.pi / plan_span)
    step_rate = 0.1 + 0.45 * (1.0 + jnp.cos(angle))
    combine(0)
    relay(1)
    raw(1)
    relay(2)
    drain(peak_row, peak_sem.at[0])
    peak_a[...] = jnp.max(peak_row[...], axis=0)
    for k in range(1, Z):
        remote(peak_a, peak_col.at[z], peak_send.at[1], peak_sem.at[1], (d, column_peer(k))).start()
    pltpu.make_async_copy(peak_a, peak_col.at[z], peak_sem.at[1]).start()

    for t in range(LAG):
        home(t)
        if t == 0:
            drain(peak_col, peak_sem.at[1])
            peak_b[...] = jnp.max(peak_col[...], axis=0)
            for other in (up, down, far):
                remote(peak_b, peak_dp.at[d], peak_send.at[2], peak_sem.at[2], (other, e)).start()
            pltpu.make_async_copy(peak_b, peak_dp.at[d], peak_sem.at[2]).start()
        combine(t + 1)
        go(t, 0, 8)
        raw(t + 2)
        go(t, 8, PER)
        relay(t + 3)

    def step(t, _):
        @pl.when(t < ROUNDS)
        def _():
            home(t)

        @pl.when(t + 1 < ROUNDS)
        def _():
            combine(t + 1)

        @pl.when(t < ROUNDS)
        def _():
            go(t, 0, 8)

        @pl.when(t + 2 < ROUNDS)
        def _():
            raw(t + 2)

        @pl.when(t < ROUNDS)
        def _():
            go(t, 8, PER)

        @pl.when(t + 3 < ROUNDS)
        def _():
            relay(t + 3)

        finish(t)
        return 0

    lax.fori_loop(LAG, ROUNDS + LAG, step, 0)

    drain(peak_dp, peak_sem.at[2])
    eta = jnp.minimum(1.0, clip_tau / jnp.max(peak_dp[...], axis=0))
    ids = jnp.transpose(jnp.broadcast_to(ids_lane[...], (SLOTS, SLOTS)))[:, 0:1]
    kind = ids % 2
    layer = ids // (2 * eta.shape[1])
    head = (ids // 2) % eta.shape[1]
    lanes = lax.broadcasted_iota(jnp.int32, (SLOTS, eta.shape[1]), 1)
    picked = jnp.zeros((SLOTS, eta.shape[1]), jnp.float32)
    for level in range(eta.shape[0]):
        picked = jnp.where(layer == level, eta[level : level + 1, :], picked)
    slot_eta = jnp.sum(jnp.where(lanes == head, picked, 0.0), axis=1, keepdims=True)
    column = lax.broadcasted_iota(jnp.int32, (SLOTS, KV_OUT), 1)
    rest = jnp.where(kind == 0, jnp.where(column < Q_OUT, slot_eta, 0.0), 1.0)
    clip_ref[...] = jnp.where(column < NOPE_DIM, jnp.sqrt(slot_eta), rest)

    def collect(r, _):
        unpack(r)
        return 0

    lax.fori_loop(0, ROUNDS, collect, 0)
    drain(peak_row.at[pl.ds(0, 2 * X - 1)], peak_send.at[0])
    drain(peak_col.at[pl.ds(0, Z - 1)], peak_send.at[1])
    drain(peak_dp.at[pl.ds(0, DP - 1)], peak_send.at[2])
    for sem in (relay_send, raw_send, sum_send):
        drain(held, sem)

    def settle(count):
        drain(nest.at[pl.ds(0, (SLOTS - 2) * count // ALL)], go_send)
        drain(back.at[pl.ds(0, 2 * (ARRIVING - count))], back_send)

    by_width(settle)


def fused_step(ids, ids_row, step, grads, momentum, logit):
    slab = (ROWS, KV_OUT)
    bf16 = jnp.bfloat16
    halves = pltpu.VMEM((ROUNDS, HALF) + slab, bf16)
    wholes = pltpu.VMEM((ROUNDS, 2, HALF) + slab, bf16)
    slots = pltpu.VMEM((SLOTS,) + slab, bf16)
    tiles = pltpu.VMEM((SLOTS, ALL, 8, 128), bf16)
    flat = pltpu.VMEM((SLOTS * ALL, 8, 128), bf16)
    heads = logit.shape
    dma = pltpu.SemaphoreType.DMA
    vmem = pl.BlockSpec(memory_space=pltpu.VMEM)
    hbm = pl.BlockSpec(memory_space=pltpu.HBM)
    return pl.pallas_call(
        step_kernel,
        in_specs=[hbm, hbm, pl.BlockSpec(memory_space=pltpu.SMEM), hbm, hbm, hbm],
        out_specs=[vmem, vmem, vmem],
        out_shape=[
            pltpu.VMEM((SLOTS,) + slab, bf16),
            pltpu.VMEM((SLOTS,) + slab, bf16),
            pltpu.VMEM((SLOTS, KV_OUT), jnp.float32),
        ],
        scratch_shapes=[
            pltpu.SMEM(ids.shape, jnp.int32),
            pltpu.VMEM(ids_row.shape, jnp.int32),
            pltpu.VMEM(heads, jnp.float32),
            wholes, halves, halves, slots, halves, halves, wholes, wholes, tiles, flat, flat, tiles,
            pltpu.VMEM((2 * X,) + heads, jnp.float32),
            pltpu.VMEM((Z,) + heads, jnp.float32),
            pltpu.VMEM((DP,) + heads, jnp.float32),
            pltpu.VMEM(heads, jnp.float32),
            pltpu.VMEM(heads, jnp.float32),
            dma((7,)), dma, dma((ROUNDS, 2)), dma, dma, dma((ROUNDS, 2)), dma, dma((2,)), dma, dma((ROUNDS,)),
            dma((3,)), dma((3,)),
        ],
        compiler_params=pltpu.CompilerParams(
            collective_id=0, has_side_effects=True, vmem_limit_bytes=40 * 2**20
        ),
    )(ids, ids_row, step, grads, momentum, logit)


def tail_kernel(fresh, update, clip, fresh_out, update_out, clip_out, sems):
    copies = [
        pltpu.make_async_copy(fresh, fresh_out, sems.at[0]),
        pltpu.make_async_copy(update, update_out, sems.at[1]),
        pltpu.make_async_copy(clip, clip_out, sems.at[2]),
    ]
    for copy in copies:
        copy.start()
    for copy in copies:
        copy.wait()


def write_out(fresh, update, clip):
    vmem = pl.BlockSpec(memory_space=pltpu.VMEM)
    anywhere = pl.BlockSpec(memory_space=pl.ANY)
    return pl.pallas_call(
        tail_kernel,
        in_specs=[vmem] * 3,
        out_specs=[anywhere] * 3,
        out_shape=[
            jax.ShapeDtypeStruct(fresh.shape, fresh.dtype),
            jax.ShapeDtypeStruct(update.shape, update.dtype),
            jax.ShapeDtypeStruct((SLOTS, KV_OUT), jnp.float32),
        ],
        scratch_shapes=[pltpu.SemaphoreType.DMA((3,))],
    )(fresh, update, clip)


def body(grad_parts, momentum, block_ids, step, logit_max):
    grads = grad_parts.reshape(DP, ROUNDS, 2, HALF, ROWS, KV_OUT)
    operands = (block_ids, block_ids.reshape(1, SLOTS), grads, momentum, logit_max[0, 0])
    ids, ids_row, grads, momentum, logit = (pltpu.with_memory_space_constraint(a, pltpu.HBM) for a in operands)
    results = fused_step(ids, ids_row, step, grads, momentum, logit)
    return tuple(write_out(*(pltpu.with_memory_space_constraint(a, pltpu.VMEM) for a in results)))


def solution(mesh):
    in_specs = (
        P("dp", None, "expert", None),
        P("dp", "expert", None),
        P("dp"),
        P(),
        P("dp", "expert", None, None),
    )
    out_specs = (P("dp", "expert", None), P("dp", "expert", None), P("dp", None))
    return jax.shard_map(body, mesh=mesh, in_specs=in_specs, out_specs=out_specs, check_vma=False)
```

```python
import math

import jax
import jax.numpy as jnp
from jax import lax
from jax.experimental import pallas as pl
from jax.experimental.pallas import tpu as pltpu
from jax.sharding import PartitionSpec as P

Q_IN = 1536
KV_IN = 512
NOPE_DIM = 128
NS_STEPS = 5
Q_OUT = 192
KV_OUT = 256
ROWS = 24
SLOTS = 128
ROUNDS = 8
PER = 16
HALF = 8
LAG = 2
PACE = 16
Z = 8
X = 4
DP = 4
FULL = -(-KV_IN // ROWS)
ALL = 6
FEW = 5
ARRIVING = FULL * ALL + (2 * X * Z - FULL) * FEW
MESH = pl.DeviceIdType.MESH

quintic_a = 3.4445
quintic_b = -4.775
quintic_c = 2.0315
norm_eps = 1e-07
beta_coef = 0.95
clip_tau = 100.0
plan_span = 10000.0
rms_match = 0.2
QUERY_SCALE = rms_match * math.sqrt(max(Q_IN, Q_OUT))
VALUE_SCALE = rms_match * math.sqrt(max(KV_IN, KV_OUT))


def split(value):
    high = value.astype(jnp.bfloat16)
    low = (value - high.astype(jnp.float32)).astype(jnp.bfloat16)
    return high, low


def dot(left, right):
    return jnp.dot(left, right, preferred_element_type=jnp.float32)


def product(left, right):
    (lh, ll), (rh, rl) = left, right
    return dot(lh, rh) + (dot(lh, rl) + dot(ll, rh))


def polar_factor(gram0):
    rows = lax.broadcasted_iota(jnp.int32, gram0.shape, 0)
    columns = lax.broadcasted_iota(jnp.int32, gram0.shape, 1)
    eye = jnp.where(rows == columns, 1.0, 0.0)
    squares = jnp.sum(jnp.sum(gram0 * eye, axis=1, keepdims=True), axis=0, keepdims=True)
    inverse = 1.0 / (jnp.sqrt(squares) + norm_eps)
    gram = (gram0 * inverse) * inverse
    factor = None
    for sweep in range(NS_STEPS):
        parts = split(gram)
        poly = quintic_a * eye + quintic_b * gram + quintic_c * product(parts, parts)
        poly_parts = split(poly)
        factor = poly if factor is None else product(split(factor), poly_parts)
        if sweep < NS_STEPS - 1:
            gram = product(split(product(parts, poly_parts)), poly_parts)
    return factor * inverse


def drain(ref, sem):
    pltpu.make_async_copy(ref, ref, sem).wait()


def step_kernel(
    ids_hbm, ids_row, step_ref, grads, momentum, logit_hbm, fresh, update, clip_ref,
    ids_ref, ids_lane, logit,
    own, near_up, near_down, held, relay_up, relay_down, in_up, in_down, nest, owned, back, returned,
    peak_row, peak_col, peak_dp, peak_a, peak_b,
    load_sem, relay_send, relay_sem, raw_send, sum_send, in_sem, go_send, go_sem, back_send, back_sem,
    peak_send, peak_sem,
):
    d = lax.axis_index("dp")
    e = lax.axis_index("expert")
    z, x, core = e // (2 * X), (e // 2) % X, e % 2
    inner = e % (2 * X)
    family = (x + z) % 2 + 2 * core
    place = 2 * z + x // 2
    up, down, far = (d + 1) % DP, (d + 3) % DP, (d + 2) % DP

    def remote(source, target, send, recv, where):
        return pltpu.make_async_remote_copy(
            src_ref=source, dst_ref=target, send_sem=send, recv_sem=recv, device_id=where, device_id_type=MESH
        )

    def row_peer(k):
        return 2 * X * z + (inner + k) % (2 * X)

    def column_peer(k):
        return 2 * X * ((z + k) % Z) + inner

    barrier = pltpu.get_barrier_semaphore()

    def greet(where):
        pl.semaphore_signal(barrier, inc=1, device_id=where, device_id_type=MESH)

    for other in (up, down, far):
        greet((other, e))
    for k in range(1, 2 * X):
        greet((d, row_peer(k)))
    for k in range(1, Z):
        greet((d, column_peer(k)))
    loads = [
        pltpu.make_async_copy(grads.at[up, :, 0], near_up, load_sem.at[0]),
        pltpu.make_async_copy(grads.at[down, :, 1], near_down, load_sem.at[1]),
        pltpu.make_async_copy(grads.at[d], own, load_sem.at[2]),
        pltpu.make_async_copy(momentum, held, load_sem.at[3]),
        pltpu.make_async_copy(ids_hbm, ids_ref, load_sem.at[4]),
        pltpu.make_async_copy(ids_row, ids_lane, load_sem.at[6]),
    ]
    load_logit = pltpu.make_async_copy(logit_hbm, logit, load_sem.at[5])
    load_logit.start()
    for load in loads:
        load.start()
    pl.semaphore_wait(barrier, DP - 1 + 2 * X - 1 + Z - 1)

    def relay(r):
        remote(grads.at[far, r, 0], relay_down.at[r], relay_send, relay_sem.at[r, 0], (up, e)).start()
        remote(grads.at[far, r, 1], relay_up.at[r], relay_send, relay_sem.at[r, 1], (down, e)).start()

    def raw(r):
        remote(grads.at[up, r, 1], in_down.at[r, 1], raw_send, in_sem.at[r, 0], (up, e)).start()
        remote(grads.at[down, r, 0], in_up.at[r, 0], raw_send, in_sem.at[r, 1], (down, e)).start()

    def combine(r):
        for side, (near, relayed) in enumerate(((near_up, relay_down), (near_down, relay_up))):
            drain(relayed.at[r], relay_sem.at[r, side])

            def add(i, _, near=near, relayed=relayed):
                near[r, i] = (near[r, i].astype(jnp.float32) + relayed[r, i].astype(jnp.float32)).astype(jnp.bfloat16)
                return 0

            lax.fori_loop(0, HALF, add, 0, unroll=True)
            if side == 0:
                remote(near_up.at[r], in_down.at[r, 0], sum_send, in_sem.at[r, 0], (up, e)).start()
            else:
                remote(near_down.at[r], in_up.at[r, 1], sum_send, in_sem.at[r, 1], (down, e)).start()

    row = e * ROWS + lax.broadcasted_iota(jnp.int32, (ROWS, KV_OUT), 0)
    column = lax.broadcasted_iota(jnp.int32, (ROWS, KV_OUT), 1)
    query_live = jnp.where(column < Q_OUT, 1.0, 0.0)
    value_live = jnp.where(row < KV_IN, 1.0, 0.0)
    lane = lax.broadcasted_iota(jnp.int32, (8, 128), 1)
    wide = e < FULL
    wide_tile = 0 * lane + e < FULL

    def by_width(act):
        @pl.when(wide)
        def _():
            act(ALL)

        @pl.when(jnp.logical_not(wide))
        def _():
            act(FEW)


    def home(r):
        drain(in_down.at[r], in_sem.at[r, 0])
        drain(in_up.at[r], in_sem.at[r, 1])
        for half in range(2):

            def one(i, _, half=half):
                slot = r * PER + half * HALF + i
                query = (1 - ids_ref[slot] % 2).astype(jnp.float32)
                live = value_live + query * (query_live - value_live)
                total = own[r, half, i].astype(jnp.float32) + (
                    in_down[r, half, i].astype(jnp.float32) + in_up[r, half, i].astype(jnp.float32)
                )
                gradient = live * total
                state = (live * (beta_coef * held[slot].astype(jnp.float32) + gradient)).astype(jnp.bfloat16)
                fresh[slot] = state
                ahead = gradient + beta_coef * state.astype(jnp.float32)
                left = ahead[:, :128].reshape(3, 8, 128)
                right = ahead[:, 128:].reshape(3, 8, 128)
                folded = jnp.where(wide_tile, right[0], right[0] + pltpu.roll(right[1], 64, 1))
                second = jnp.where(wide_tile, right[1], right[2])
                tiles = jnp.concatenate([left, folded[None], second[None], right[2:3]], axis=0)
                nest[slot] = tiles.astype(jnp.bfloat16)
                return 0

            lax.fori_loop(0, HALF, one, 0, unroll=True)

    def go(r, low, high):
        owner = r % 4
        first = (r // 4) * 2 * X * Z * ALL + e * ALL

        def route(k):
            to_z = (z + k % Z) % Z
            to_half = (x // 2 + k // Z) % 2
            target = 2 * (X * to_z + 2 * to_half + (owner + to_z) % 2) + owner // 2
            return r * PER + 2 * to_z + to_half, target

        def push(count):
            arriving = owned.at[pl.ds(first, count)]

            def send(k, _):
                slot, target = route(k)
                remote(nest.at[slot, pl.ds(0, count)], arriving, go_send, go_sem.at[r // 4], (d, target)).start()
                return 0

            lax.fori_loop(max(low, 1), high, send, 0)
            if low > 0:
                return

            @pl.when(owner == family)
            def _():
                pltpu.make_async_copy(nest.at[r * PER + place, pl.ds(0, count)], arriving, go_sem.at[r // 4]).start()

            @pl.when(owner != family)
            def _():
                send(0, 0)

        by_width(push)

    def orthogonalize(r):
        j = r // 4
        query = (1 - ids_ref[r * PER + place] % 2).astype(jnp.float32)
        width = VALUE_SCALE + query * (QUERY_SCALE - VALUE_SCALE)
        base = j * 2 * X * Z * ALL
        drain(owned.at[pl.ds(base, ARRIVING)], go_sem.at[j])
        tiles = owned[pl.ds(base, 2 * X * Z * ALL)].astype(jnp.float32).reshape(2 * X * Z, ALL, 8, 128)
        half = lax.broadcasted_iota(jnp.int32, (2 * X * Z - FULL, 8, 128), 2) < 64
        folded = tiles[FULL:, 3]
        narrow = [
            jnp.where(half, folded, 0.0),
            jnp.where(half, pltpu.roll(folded, 64, 2), 0.0),
            tiles[FULL:, 4],
        ]
        right = jnp.concatenate([tiles[:FULL, 3:], jnp.stack(narrow, axis=1)], axis=0)
        parts = [tiles[:, :3].reshape(Q_IN, 128), right.reshape(Q_IN, 128)]
        rows = jnp.concatenate(parts, axis=1).astype(jnp.bfloat16)
        gram0 = lax.dot_general(rows, rows, (((0,), (0,)), ((), ())), preferred_element_type=jnp.float32)
        factor = polar_factor(gram0) * (width * step_rate)
        high, low = split(factor)
        result = dot(rows, high) + dot(rows, low)
        left = result[:, :128].reshape(2 * X * Z, 3, 8, 128)
        right = result[:, 128:].reshape(2 * X * Z, 3, 8, 128)
        narrow = right[FULL:]
        folded = jnp.where(half, narrow[:, 0], pltpu.roll(narrow[:, 1], 64, 2))
        packed = jnp.stack([folded, narrow[:, 2], narrow[:, 2]], axis=1)
        tiles = jnp.concatenate([left, jnp.concatenate([right[:FULL], packed], axis=0)], axis=1)
        back[pl.ds(base, 2 * X * Z * ALL)] = tiles.reshape(2 * X * Z * ALL, 8, 128).astype(jnp.bfloat16)

    def give(j, first, last):
        slot = (4 * j + family) * PER + place

        def send(k, _):
            target = 2 * X * ((z + k % Z) % Z) + (inner + k // Z) % (2 * X)

            def push(count):
                remote(
                    back.at[pl.ds((j * 2 * X * Z + target) * ALL, count)], returned.at[slot, pl.ds(0, count)],
                    back_send, back_sem.at[4 * j + family], (d, target),
                ).start()

            @pl.when(target < FULL)
            def _():
                push(ALL)

            @pl.when(target >= FULL)
            def _():
                push(FEW)

            return 0

        lax.fori_loop(first, last, send, 0)

    def keep(r):
        def move(count):
            pltpu.make_async_copy(
                back.at[pl.ds(((r // 4) * 2 * X * Z + e) * ALL, count)],
                returned.at[r * PER + place, pl.ds(0, count)],
                back_sem.at[r],
            ).start()

        by_width(move)

    def unpack(r):
        drain_rows = pl.ds(r * PER, PER)

        @pl.when(wide)
        def _():
            drain(returned.at[drain_rows], back_sem.at[r])

            def one(i, _):
                tiles = returned[r * PER + i].astype(jnp.float32)
                update[r * PER + i] = jnp.concatenate(
                    [tiles[:3].reshape(ROWS, 128), tiles[3:].reshape(ROWS, 128)], axis=1
                ).astype(jnp.bfloat16)
                return 0

            lax.fori_loop(0, PER, one, 0, unroll=4)

        @pl.when(jnp.logical_not(wide))
        def _():
            drain(returned.at[drain_rows, pl.ds(0, FEW)], back_sem.at[r])

            def one(i, _):
                tiles = returned[r * PER + i, pl.ds(0, FEW)].astype(jnp.float32)
                first = jnp.where(lane < 64, tiles[3], 0.0)
                second = jnp.where(lane < 64, pltpu.roll(tiles[3], 64, 1), 0.0)
                right = jnp.concatenate([first, second, tiles[4]], axis=0)
                update[r * PER + i] = jnp.concatenate(
                    [tiles[:3].reshape(ROWS, 128), right], axis=1
                ).astype(jnp.bfloat16)
                return 0

            lax.fori_loop(0, PER, one, 0, unroll=4)

    def given(t, start):
        paced = jnp.minimum(jnp.maximum(1 + (t - start + 1) * PACE, 1), 2 * X * Z)
        return jnp.where(t < ROUNDS, paced, jnp.where(t < start, 1, 2 * X * Z))

    starts = (LAG + family - jnp.where(family < 2, 1, 0), LAG + 5 + family)

    def finish(t):
        @pl.when((t == starts[0]) | (t == starts[1]))
        def _():
            r = 4 * jnp.where(t == starts[1], 1, 0) + family
            orthogonalize(r)
            keep(r)

        for j in range(2):
            start = starts[j]
            give(j, given(t - 1, start), given(t, start))

    relay(0)
    raw(0)
    load_logit.wait()
    for k in range(1, 2 * X):
        remote(logit, peak_row.at[inner], peak_send.at[0], peak_sem.at[0], (d, row_peer(k))).start()
    pltpu.make_async_copy(logit, peak_row.at[inner], peak_sem.at[0]).start()
    for load in loads[:2]:
        load.wait()
    angle = jnp.full((1, KV_OUT), step_ref[0], jnp.int32).astype(jnp.float32) * (math.pi / plan_span)
    step_rate = 0.1 + 0.45 * (1.0 + jnp.cos(angle))
    combine(0)
    relay(1)
    raw(1)
    relay(2)
    drain(peak_row, peak_sem.at[0])
    peak_a[...] = jnp.max(peak_row[...], axis=0)
    for k in range(1, Z):
        remote(peak_a, peak_col.at[z], peak_send.at[1], peak_sem.at[1], (d, column_peer(k))).start()
    pltpu.make_async_copy(peak_a, peak_col.at[z], peak_sem.at[1]).start()

    for load in loads[2:]:
        load.wait()
    for t in range(1):
        home(t)
        if t == 0:
            drain(peak_col, peak_sem.at[1])
            peak_b[...] = jnp.max(peak_col[...], axis=0)
            for other in (up, down, far):
                remote(peak_b, peak_dp.at[d], peak_send.at[2], peak_sem.at[2], (other, e)).start()
            pltpu.make_async_copy(peak_b, peak_dp.at[d], peak_sem.at[2]).start()
        combine(t + 1)
        go(t, 0, 8)
        raw(t + 2)
        go(t, 8, PER)
        relay(t + 3)

    def step(t, _):
        @pl.when(t < ROUNDS)
        def _():
            home(t)

        @pl.when(t + 1 < ROUNDS)
        def _():
            combine(t + 1)

        @pl.when(t < ROUNDS)
        def _():
            go(t, 0, 8)

        @pl.when(t + 2 < ROUNDS)
        def _():
            raw(t + 2)

        @pl.when(t < ROUNDS)
        def _():
            go(t, 8, PER)

        @pl.when(t + 3 < ROUNDS)
        def _():
            relay(t + 3)

        finish(t)
        return 0

    lax.fori_loop(1, ROUNDS + LAG + 1, step, 0)

    drain(peak_dp, peak_sem.at[2])
    eta = jnp.minimum(1.0, clip_tau / jnp.max(peak_dp[...], axis=0))
    ids = jnp.transpose(jnp.broadcast_to(ids_lane[...], (SLOTS, SLOTS)))[:, 0:1]
    kind = ids % 2
    layer = ids // (2 * eta.shape[1])
    head = (ids // 2) % eta.shape[1]
    lanes = lax.broadcasted_iota(jnp.int32, (SLOTS, eta.shape[1]), 1)
    picked = jnp.zeros((SLOTS, eta.shape[1]), jnp.float32)
    for level in range(eta.shape[0]):
        picked = jnp.where(layer == level, eta[level : level + 1, :], picked)
    slot_eta = jnp.sum(jnp.where(lanes == head, picked, 0.0), axis=1, keepdims=True)
    column = lax.broadcasted_iota(jnp.int32, (SLOTS, KV_OUT), 1)
    rest = jnp.where(kind == 0, jnp.where(column < Q_OUT, slot_eta, 0.0), 1.0)
    clip_ref[...] = jnp.where(column < NOPE_DIM, jnp.sqrt(slot_eta), rest)

    def collect(r, _):
        unpack(r)
        return 0

    lax.fori_loop(0, ROUNDS, collect, 0)
    drain(peak_row.at[pl.ds(0, 2 * X - 1)], peak_send.at[0])
    drain(peak_col.at[pl.ds(0, Z - 1)], peak_send.at[1])
    drain(peak_dp.at[pl.ds(0, DP - 1)], peak_send.at[2])
    for sem in (relay_send, raw_send, sum_send):
        drain(held, sem)

    def settle(count):
        drain(nest.at[pl.ds(0, (SLOTS - 2) * count // ALL)], go_send)
        drain(back.at[pl.ds(0, 2 * (ARRIVING - count))], back_send)

    by_width(settle)


def fused_step(ids, ids_row, step, grads, momentum, logit):
    slab = (ROWS, KV_OUT)
    bf16 = jnp.bfloat16
    halves = pltpu.VMEM((ROUNDS, HALF) + slab, bf16)
    wholes = pltpu.VMEM((ROUNDS, 2, HALF) + slab, bf16)
    slots = pltpu.VMEM((SLOTS,) + slab, bf16)
    tiles = pltpu.VMEM((SLOTS, ALL, 8, 128), bf16)
    flat = pltpu.VMEM((SLOTS * ALL, 8, 128), bf16)
    heads = logit.shape
    dma = pltpu.SemaphoreType.DMA
    vmem = pl.BlockSpec(memory_space=pltpu.VMEM)
    hbm = pl.BlockSpec(memory_space=pltpu.HBM)
    return pl.pallas_call(
        step_kernel,
        in_specs=[hbm, hbm, pl.BlockSpec(memory_space=pltpu.SMEM), hbm, hbm, hbm],
        out_specs=[vmem, vmem, vmem],
        out_shape=[
            pltpu.VMEM((SLOTS,) + slab, bf16),
            pltpu.VMEM((SLOTS,) + slab, bf16),
            pltpu.VMEM((SLOTS, KV_OUT), jnp.float32),
        ],
        scratch_shapes=[
            pltpu.SMEM(ids.shape, jnp.int32),
            pltpu.VMEM(ids_row.shape, jnp.int32),
            pltpu.VMEM(heads, jnp.float32),
            wholes, halves, halves, slots, halves, halves, wholes, wholes, tiles, flat, flat, tiles,
            pltpu.VMEM((2 * X,) + heads, jnp.float32),
            pltpu.VMEM((Z,) + heads, jnp.float32),
            pltpu.VMEM((DP,) + heads, jnp.float32),
            pltpu.VMEM(heads, jnp.float32),
            pltpu.VMEM(heads, jnp.float32),
            dma((7,)), dma, dma((ROUNDS, 2)), dma, dma, dma((ROUNDS, 2)), dma, dma((2,)), dma, dma((ROUNDS,)),
            dma((3,)), dma((3,)),
        ],
        compiler_params=pltpu.CompilerParams(
            collective_id=0, has_side_effects=True, vmem_limit_bytes=40 * 2**20
        ),
    )(ids, ids_row, step, grads, momentum, logit)


def tail_kernel(fresh, update, clip, fresh_out, update_out, clip_out, sems):
    copies = [
        pltpu.make_async_copy(fresh, fresh_out, sems.at[0]),
        pltpu.make_async_copy(update, update_out, sems.at[1]),
        pltpu.make_async_copy(clip, clip_out, sems.at[2]),
    ]
    for copy in copies:
        copy.start()
    for copy in copies:
        copy.wait()


def write_out(fresh, update, clip):
    vmem = pl.BlockSpec(memory_space=pltpu.VMEM)
    anywhere = pl.BlockSpec(memory_space=pl.ANY)
    return pl.pallas_call(
        tail_kernel,
        in_specs=[vmem] * 3,
        out_specs=[anywhere] * 3,
        out_shape=[
            jax.ShapeDtypeStruct(fresh.shape, fresh.dtype),
            jax.ShapeDtypeStruct(update.shape, update.dtype),
            jax.ShapeDtypeStruct((SLOTS, KV_OUT), jnp.float32),
        ],
        scratch_shapes=[pltpu.SemaphoreType.DMA((3,))],
    )(fresh, update, clip)


def body(grad_parts, momentum, block_ids, step, logit_max):
    grads = grad_parts.reshape(DP, ROUNDS, 2, HALF, ROWS, KV_OUT)
    operands = (block_ids, block_ids.reshape(1, SLOTS), grads, momentum, logit_max[0, 0])
    ids, ids_row, grads, momentum, logit = (pltpu.with_memory_space_constraint(a, pltpu.HBM) for a in operands)
    results = fused_step(ids, ids_row, step, grads, momentum, logit)
    return tuple(write_out(*(pltpu.with_memory_space_constraint(a, pltpu.VMEM) for a in results)))


def solution(mesh):
    in_specs = (
        P("dp", None, "expert", None),
        P("dp", "expert", None),
        P("dp"),
        P(),
        P("dp", "expert", None, None),
    )
    out_specs = (P("dp", "expert", None), P("dp", "expert", None), P("dp", None))
    return jax.shard_map(body, mesh=mesh, in_specs=in_specs, out_specs=out_specs, check_vma=False)
```

```python
import math

import jax
import jax.numpy as jnp
from jax import lax
from jax.experimental import pallas as pl
from jax.experimental.pallas import tpu as pltpu
from jax.sharding import PartitionSpec as P

Q_IN = 1536
KV_IN = 512
NOPE_DIM = 128
NS_STEPS = 5
Q_OUT = 192
KV_OUT = 256
ROWS = 24
SLOTS = 128
ROUNDS = 8
PER = 16
HALF = 8
LAG = 2
PACE = 16
Z = 8
X = 4
DP = 4
FULL = -(-KV_IN // ROWS)
ALL = 6
FEW = 5
ARRIVING = FULL * ALL + (2 * X * Z - FULL) * FEW
MESH = pl.DeviceIdType.MESH

quintic_a = 3.4445
quintic_b = -4.775
quintic_c = 2.0315
norm_eps = 1e-07
beta_coef = 0.95
clip_tau = 100.0
plan_span = 10000.0
rms_match = 0.2
QUERY_SCALE = rms_match * math.sqrt(max(Q_IN, Q_OUT))
VALUE_SCALE = rms_match * math.sqrt(max(KV_IN, KV_OUT))


def split(value):
    high = value.astype(jnp.bfloat16)
    low = (value - high.astype(jnp.float32)).astype(jnp.bfloat16)
    return high, low


def dot(left, right):
    return jnp.dot(left, right, preferred_element_type=jnp.float32)


def product(left, right):
    (lh, ll), (rh, rl) = left, right
    return dot(lh, rh) + (dot(lh, rl) + dot(ll, rh))


def polar_factor(gram0):
    rows = lax.broadcasted_iota(jnp.int32, gram0.shape, 0)
    columns = lax.broadcasted_iota(jnp.int32, gram0.shape, 1)
    eye = jnp.where(rows == columns, 1.0, 0.0)
    squares = jnp.sum(jnp.sum(gram0 * eye, axis=1, keepdims=True), axis=0, keepdims=True)
    inverse = 1.0 / (jnp.sqrt(squares) + norm_eps)
    gram = (gram0 * inverse) * inverse
    factor = None
    for sweep in range(NS_STEPS):
        parts = split(gram)
        poly = quintic_a * eye + quintic_b * gram + quintic_c * product(parts, parts)
        poly_parts = split(poly)
        factor = poly if factor is None else product(split(factor), poly_parts)
        if sweep < NS_STEPS - 1:
            gram = product(split(product(parts, poly_parts)), poly_parts)
    return factor * inverse


def drain(ref, sem):
    pltpu.make_async_copy(ref, ref, sem).wait()


def step_kernel(
    ids_hbm, ids_row, step_ref, grads, momentum, logit_hbm, fresh, update, clip_ref,
    ids_ref, ids_lane, logit,
    own, near_up, near_down, held, relay_up, relay_down, in_up, in_down, nest, owned, back, returned,
    peak_row, peak_col, peak_dp, peak_a, peak_b,
    load_sem, relay_send, relay_sem, raw_send, sum_send, in_sem, go_send, go_sem, back_send, back_sem,
    peak_send, peak_sem,
):
    d = lax.axis_index("dp")
    e = lax.axis_index("expert")
    z, x, core = e // (2 * X), (e // 2) % X, e % 2
    inner = e % (2 * X)
    family = (x + z) % 2 + 2 * core
    place = 2 * z + x // 2
    up, down, far = (d + 1) % DP, (d + 3) % DP, (d + 2) % DP

    def remote(source, target, send, recv, where):
        return pltpu.make_async_remote_copy(
            src_ref=source, dst_ref=target, send_sem=send, recv_sem=recv, device_id=where, device_id_type=MESH
        )

    def row_peer(k):
        return 2 * X * z + (inner + k) % (2 * X)

    def column_peer(k):
        return 2 * X * ((z + k) % Z) + inner

    barrier = pltpu.get_barrier_semaphore()

    def greet(where):
        pl.semaphore_signal(barrier, inc=1, device_id=where, device_id_type=MESH)

    for other in (up, down, far):
        greet((other, e))
    for k in range(1, 2 * X):
        greet((d, row_peer(k)))
    for k in range(1, Z):
        greet((d, column_peer(k)))
    loads = [
        pltpu.make_async_copy(grads.at[up, :, 0], near_up, load_sem.at[0]),
        pltpu.make_async_copy(grads.at[down, :, 1], near_down, load_sem.at[1]),
        pltpu.make_async_copy(grads.at[d], own, load_sem.at[2]),
        pltpu.make_async_copy(momentum, held, load_sem.at[3]),
        pltpu.make_async_copy(ids_hbm, ids_ref, load_sem.at[4]),
        pltpu.make_async_copy(ids_row, ids_lane, load_sem.at[6]),
    ]
    load_logit = pltpu.make_async_copy(logit_hbm, logit, load_sem.at[5])
    load_logit.start()
    for load in loads:
        load.start()
    pl.semaphore_wait(barrier, DP - 1 + 2 * X - 1 + Z - 1)

    def relay(r):
        remote(grads.at[far, r, 0], relay_down.at[r], relay_send, relay_sem.at[r, 0], (up, e)).start()
        remote(grads.at[far, r, 1], relay_up.at[r], relay_send, relay_sem.at[r, 1], (down, e)).start()

    def raw(r):
        remote(grads.at[up, r, 1], in_down.at[r, 1], raw_send, in_sem.at[r, 0], (up, e)).start()
        remote(grads.at[down, r, 0], in_up.at[r, 0], raw_send, in_sem.at[r, 1], (down, e)).start()

    def combine(r):
        for side, (near, relayed) in enumerate(((near_up, relay_down), (near_down, relay_up))):
            drain(relayed.at[r], relay_sem.at[r, side])

            def add(i, _, near=near, relayed=relayed):
                near[r, i] = (near[r, i].astype(jnp.float32) + relayed[r, i].astype(jnp.float32)).astype(jnp.bfloat16)
                return 0

            lax.fori_loop(0, HALF, add, 0, unroll=True)
            if side == 0:
                remote(near_up.at[r], in_down.at[r, 0], sum_send, in_sem.at[r, 0], (up, e)).start()
            else:
                remote(near_down.at[r], in_up.at[r, 1], sum_send, in_sem.at[r, 1], (down, e)).start()

    row = e * ROWS + lax.broadcasted_iota(jnp.int32, (ROWS, KV_OUT), 0)
    column = lax.broadcasted_iota(jnp.int32, (ROWS, KV_OUT), 1)
    query_live = jnp.where(column < Q_OUT, 1.0, 0.0)
    value_live = jnp.where(row < KV_IN, 1.0, 0.0)
    lane = lax.broadcasted_iota(jnp.int32, (8, 128), 1)
    wide = e < FULL
    wide_tile = 0 * lane + e < FULL

    def by_width(act):
        @pl.when(wide)
        def _():
            act(ALL)

        @pl.when(jnp.logical_not(wide))
        def _():
            act(FEW)


    def home(r):
        drain(in_down.at[r], in_sem.at[r, 0])
        drain(in_up.at[r], in_sem.at[r, 1])
        for half in range(2):

            def one(i, _, half=half):
                slot = r * PER + half * HALF + i
                query = (1 - ids_ref[slot] % 2).astype(jnp.float32)
                live = value_live + query * (query_live - value_live)
                total = own[r, half, i].astype(jnp.float32) + (
                    in_down[r, half, i].astype(jnp.float32) + in_up[r, half, i].astype(jnp.float32)
                )
                gradient = live * total
                state = (live * (beta_coef * held[slot].astype(jnp.float32) + gradient)).astype(jnp.bfloat16)
                fresh[slot] = state
                ahead = gradient + beta_coef * state.astype(jnp.float32)
                left = ahead[:, :128].reshape(3, 8, 128)
                right = ahead[:, 128:].reshape(3, 8, 128)
                folded = jnp.where(wide_tile, right[0], right[0] + pltpu.roll(right[1], 64, 1))
                second = jnp.where(wide_tile, right[1], right[2])
                tiles = jnp.concatenate([left, folded[None], second[None], right[2:3]], axis=0)
                nest[slot] = tiles.astype(jnp.bfloat16)
                return 0

            lax.fori_loop(0, HALF, one, 0, unroll=True)

    def go(r, low, high):
        owner = r % 4
        first = (r // 4) * 2 * X * Z * ALL + e * ALL

        def route(k):
            to_z = (z + k % Z) % Z
            to_half = (x // 2 + k // Z) % 2
            target = 2 * (X * to_z + 2 * to_half + (owner + to_z) % 2) + owner // 2
            return r * PER + 2 * to_z + to_half, target

        def push(count):
            arriving = owned.at[pl.ds(first, count)]

            def send(k, _):
                slot, target = route(k)
                remote(nest.at[slot, pl.ds(0, count)], arriving, go_send, go_sem.at[r // 4], (d, target)).start()
                return 0

            lax.fori_loop(max(low, 1), high, send, 0, unroll=True)
            if low > 0:
                return

            @pl.when(owner == family)
            def _():
                pltpu.make_async_copy(nest.at[r * PER + place, pl.ds(0, count)], arriving, go_sem.at[r // 4]).start()

            @pl.when(owner != family)
            def _():
                send(0, 0)

        by_width(push)

    def orthogonalize(r):
        j = r // 4
        query = (1 - ids_ref[r * PER + place] % 2).astype(jnp.float32)
        width = VALUE_SCALE + query * (QUERY_SCALE - VALUE_SCALE)
        base = j * 2 * X * Z * ALL
        drain(owned.at[pl.ds(base, ARRIVING)], go_sem.at[j])
        tiles = owned[pl.ds(base, 2 * X * Z * ALL)].astype(jnp.float32).reshape(2 * X * Z, ALL, 8, 128)
        half = lax.broadcasted_iota(jnp.int32, (2 * X * Z - FULL, 8, 128), 2) < 64
        folded = tiles[FULL:, 3]
        narrow = [
            jnp.where(half, folded, 0.0),
            jnp.where(half, pltpu.roll(folded, 64, 2), 0.0),
            tiles[FULL:, 4],
        ]
        right = jnp.concatenate([tiles[:FULL, 3:], jnp.stack(narrow, axis=1)], axis=0)
        parts = [tiles[:, :3].reshape(Q_IN, 128), right.reshape(Q_IN, 128)]
        rows = jnp.concatenate(parts, axis=1).astype(jnp.bfloat16)
        gram0 = lax.dot_general(rows, rows, (((0,), (0,)), ((), ())), preferred_element_type=jnp.float32)
        factor = polar_factor(gram0) * (width * step_rate)
        high, low = split(factor)
        result = dot(rows, high) + dot(rows, low)
        left = result[:, :128].reshape(2 * X * Z, 3, 8, 128)
        right = result[:, 128:].reshape(2 * X * Z, 3, 8, 128)
        narrow = right[FULL:]
        folded = jnp.where(half, narrow[:, 0], pltpu.roll(narrow[:, 1], 64, 2))
        packed = jnp.stack([folded, narrow[:, 2], narrow[:, 2]], axis=1)
        tiles = jnp.concatenate([left, jnp.concatenate([right[:FULL], packed], axis=0)], axis=1)
        back[pl.ds(base, 2 * X * Z * ALL)] = tiles.reshape(2 * X * Z * ALL, 8, 128).astype(jnp.bfloat16)

    def give(j, first, last):
        slot = (4 * j + family) * PER + place

        def send(k, _):
            target = 2 * X * ((z + k % Z) % Z) + (inner + k // Z) % (2 * X)

            def push(count):
                remote(
                    back.at[pl.ds((j * 2 * X * Z + target) * ALL, count)], returned.at[slot, pl.ds(0, count)],
                    back_send, back_sem.at[4 * j + family], (d, target),
                ).start()

            @pl.when(target < FULL)
            def _():
                push(ALL)

            @pl.when(target >= FULL)
            def _():
                push(FEW)

            return 0

        lax.fori_loop(first, last, send, 0)

    def keep(r):
        def move(count):
            pltpu.make_async_copy(
                back.at[pl.ds(((r // 4) * 2 * X * Z + e) * ALL, count)],
                returned.at[r * PER + place, pl.ds(0, count)],
                back_sem.at[r],
            ).start()

        by_width(move)

    def unpack(r):
        drain_rows = pl.ds(r * PER, PER)

        @pl.when(wide)
        def _():
            drain(returned.at[drain_rows], back_sem.at[r])

            def one(i, _):
                tiles = returned[r * PER + i].astype(jnp.float32)
                update[r * PER + i] = jnp.concatenate(
                    [tiles[:3].reshape(ROWS, 128), tiles[3:].reshape(ROWS, 128)], axis=1
                ).astype(jnp.bfloat16)
                return 0

            lax.fori_loop(0, PER, one, 0, unroll=4)

        @pl.when(jnp.logical_not(wide))
        def _():
            drain(returned.at[drain_rows, pl.ds(0, FEW)], back_sem.at[r])

            def one(i, _):
                tiles = returned[r * PER + i, pl.ds(0, FEW)].astype(jnp.float32)
                first = jnp.where(lane < 64, tiles[3], 0.0)
                second = jnp.where(lane < 64, pltpu.roll(tiles[3], 64, 1), 0.0)
                right = jnp.concatenate([first, second, tiles[4]], axis=0)
                update[r * PER + i] = jnp.concatenate(
                    [tiles[:3].reshape(ROWS, 128), right], axis=1
                ).astype(jnp.bfloat16)
                return 0

            lax.fori_loop(0, PER, one, 0, unroll=4)

    def given(t, start):
        paced = jnp.minimum(jnp.maximum(1 + (t - start + 1) * PACE, 1), 2 * X * Z)
        return jnp.where(t < ROUNDS, paced, jnp.where(t < start, 1, 2 * X * Z))

    starts = (LAG + family - jnp.where(family < 2, 1, 0), LAG + 5 + family)

    def finish(t):
        @pl.when((t == starts[0]) | (t == starts[1]))
        def _():
            r = 4 * jnp.where(t == starts[1], 1, 0) + family
            orthogonalize(r)
            keep(r)

        for j in range(2):
            start = starts[j]
            give(j, given(t - 1, start), given(t, start))

    relay(0)
    raw(0)
    load_logit.wait()
    for k in range(1, 2 * X):
        remote(logit, peak_row.at[inner], peak_send.at[0], peak_sem.at[0], (d, row_peer(k))).start()
    pltpu.make_async_copy(logit, peak_row.at[inner], peak_sem.at[0]).start()
    for load in loads[:2]:
        load.wait()
    angle = jnp.full((1, KV_OUT), step_ref[0], jnp.int32).astype(jnp.float32) * (math.pi / plan_span)
    step_rate = 0.1 + 0.45 * (1.0 + jnp.cos(angle))
    combine(0)
    relay(1)
    raw(1)
    relay(2)
    drain(peak_row, peak_sem.at[0])
    peak_a[...] = jnp.max(peak_row[...], axis=0)
    for k in range(1, Z):
        remote(peak_a, peak_col.at[z], peak_send.at[1], peak_sem.at[1], (d, column_peer(k))).start()
    pltpu.make_async_copy(peak_a, peak_col.at[z], peak_sem.at[1]).start()

    for load in loads[2:]:
        load.wait()
    for t in range(1):
        home(t)
        if t == 0:
            drain(peak_col, peak_sem.at[1])
            peak_b[...] = jnp.max(peak_col[...], axis=0)
            for other in (up, down, far):
                remote(peak_b, peak_dp.at[d], peak_send.at[2], peak_sem.at[2], (other, e)).start()
            pltpu.make_async_copy(peak_b, peak_dp.at[d], peak_sem.at[2]).start()
        go(t, 0, 8)
        combine(t + 1)
        raw(t + 2)
        go(t, 8, PER)
        relay(t + 3)

    def step(t, _):
        @pl.when(t < ROUNDS)
        def _():
            home(t)

        @pl.when(t < ROUNDS)
        def _():
            go(t, 0, 8)

        @pl.when(t + 1 < ROUNDS)
        def _():
            combine(t + 1)

        @pl.when(t + 2 < ROUNDS)
        def _():
            raw(t + 2)

        @pl.when(t < ROUNDS)
        def _():
            go(t, 8, PER)

        @pl.when(t + 3 < ROUNDS)
        def _():
            relay(t + 3)

        finish(t)
        return 0

    lax.fori_loop(1, ROUNDS + LAG + 1, step, 0)

    drain(peak_dp, peak_sem.at[2])
    eta = jnp.minimum(1.0, clip_tau / jnp.max(peak_dp[...], axis=0))
    ids = jnp.transpose(jnp.broadcast_to(ids_lane[...], (SLOTS, SLOTS)))[:, 0:1]
    kind = ids % 2
    layer = ids // (2 * eta.shape[1])
    head = (ids // 2) % eta.shape[1]
    lanes = lax.broadcasted_iota(jnp.int32, (SLOTS, eta.shape[1]), 1)
    picked = jnp.zeros((SLOTS, eta.shape[1]), jnp.float32)
    for level in range(eta.shape[0]):
        picked = jnp.where(layer == level, eta[level : level + 1, :], picked)
    slot_eta = jnp.sum(jnp.where(lanes == head, picked, 0.0), axis=1, keepdims=True)
    column = lax.broadcasted_iota(jnp.int32, (SLOTS, KV_OUT), 1)
    rest = jnp.where(kind == 0, jnp.where(column < Q_OUT, slot_eta, 0.0), 1.0)
    clip_ref[...] = jnp.where(column < NOPE_DIM, jnp.sqrt(slot_eta), rest)

    def collect(r, _):
        unpack(r)
        return 0

    lax.fori_loop(0, ROUNDS, collect, 0)
    drain(peak_row.at[pl.ds(0, 2 * X - 1)], peak_send.at[0])
    drain(peak_col.at[pl.ds(0, Z - 1)], peak_send.at[1])
    drain(peak_dp.at[pl.ds(0, DP - 1)], peak_send.at[2])
    for sem in (relay_send, raw_send, sum_send):
        drain(held, sem)

    def settle(count):
        drain(nest.at[pl.ds(0, (SLOTS - 2) * count // ALL)], go_send)
        drain(back.at[pl.ds(0, 2 * (ARRIVING - count))], back_send)

    by_width(settle)


def fused_step(ids, ids_row, step, grads, momentum, logit):
    slab = (ROWS, KV_OUT)
    bf16 = jnp.bfloat16
    halves = pltpu.VMEM((ROUNDS, HALF) + slab, bf16)
    wholes = pltpu.VMEM((ROUNDS, 2, HALF) + slab, bf16)
    slots = pltpu.VMEM((SLOTS,) + slab, bf16)
    tiles = pltpu.VMEM((SLOTS, ALL, 8, 128), bf16)
    flat = pltpu.VMEM((SLOTS * ALL, 8, 128), bf16)
    heads = logit.shape
    dma = pltpu.SemaphoreType.DMA
    vmem = pl.BlockSpec(memory_space=pltpu.VMEM)
    hbm = pl.BlockSpec(memory_space=pltpu.HBM)
    return pl.pallas_call(
        step_kernel,
        in_specs=[hbm, hbm, pl.BlockSpec(memory_space=pltpu.SMEM), hbm, hbm, hbm],
        out_specs=[vmem, vmem, vmem],
        out_shape=[
            pltpu.VMEM((SLOTS,) + slab, bf16),
            pltpu.VMEM((SLOTS,) + slab, bf16),
            pltpu.VMEM((SLOTS, KV_OUT), jnp.float32),
        ],
        scratch_shapes=[
            pltpu.SMEM(ids.shape, jnp.int32),
            pltpu.VMEM(ids_row.shape, jnp.int32),
            pltpu.VMEM(heads, jnp.float32),
            wholes, halves, halves, slots, halves, halves, wholes, wholes, tiles, flat, flat, tiles,
            pltpu.VMEM((2 * X,) + heads, jnp.float32),
            pltpu.VMEM((Z,) + heads, jnp.float32),
            pltpu.VMEM((DP,) + heads, jnp.float32),
            pltpu.VMEM(heads, jnp.float32),
            pltpu.VMEM(heads, jnp.float32),
            dma((7,)), dma, dma((ROUNDS, 2)), dma, dma, dma((ROUNDS, 2)), dma, dma((2,)), dma, dma((ROUNDS,)),
            dma((3,)), dma((3,)),
        ],
        compiler_params=pltpu.CompilerParams(
            collective_id=0, has_side_effects=True, vmem_limit_bytes=40 * 2**20
        ),
    )(ids, ids_row, step, grads, momentum, logit)


def tail_kernel(fresh, update, clip, fresh_out, update_out, clip_out, sems):
    copies = [
        pltpu.make_async_copy(fresh, fresh_out, sems.at[0]),
        pltpu.make_async_copy(update, update_out, sems.at[1]),
        pltpu.make_async_copy(clip, clip_out, sems.at[2]),
    ]
    for copy in copies:
        copy.start()
    for copy in copies:
        copy.wait()


def write_out(fresh, update, clip):
    vmem = pl.BlockSpec(memory_space=pltpu.VMEM)
    anywhere = pl.BlockSpec(memory_space=pl.ANY)
    return pl.pallas_call(
        tail_kernel,
        in_specs=[vmem] * 3,
        out_specs=[anywhere] * 3,
        out_shape=[
            jax.ShapeDtypeStruct(fresh.shape, fresh.dtype),
            jax.ShapeDtypeStruct(update.shape, update.dtype),
            jax.ShapeDtypeStruct((SLOTS, KV_OUT), jnp.float32),
        ],
        scratch_shapes=[pltpu.SemaphoreType.DMA((3,))],
    )(fresh, update, clip)


def body(grad_parts, momentum, block_ids, step, logit_max):
    grads = grad_parts.reshape(DP, ROUNDS, 2, HALF, ROWS, KV_OUT)
    operands = (block_ids, block_ids.reshape(1, SLOTS), grads, momentum, logit_max[0, 0])
    ids, ids_row, grads, momentum, logit = (pltpu.with_memory_space_constraint(a, pltpu.HBM) for a in operands)
    results = fused_step(ids, ids_row, step, grads, momentum, logit)
    return tuple(write_out(*(pltpu.with_memory_space_constraint(a, pltpu.VMEM) for a in results)))


def solution(mesh):
    in_specs = (
        P("dp", None, "expert", None),
        P("dp", "expert", None),
        P("dp"),
        P(),
        P("dp", "expert", None, None),
    )
    out_specs = (P("dp", "expert", None), P("dp", "expert", None), P("dp", None))
    return jax.shard_map(body, mesh=mesh, in_specs=in_specs, out_specs=out_specs, check_vma=False)
```
